256 devices in a mesh: dp: 16 (over y_lo, x, core), ref: 16 (over z, y_hi).
Axes of the slice: x: 4, y: 4 (y_hi: 2, y_lo: 2; y = y_hi * 2 + y_lo), z: 8, core: 2. Of those that a mesh axis runs over, the one named last changes fastest.
Arguments:
- images: bfloat16 [12288, 16384], P(('dp', 'ref'))
- ctf: bfloat16 [12288, 8192], P(('dp', 'ref'))
- refs: bfloat16 [192, 16384], P('ref')
- shifts: int32 [9, 2], replicated, may hold values from -3 to 3
- lists: int32 [12288, 12], P(('dp', 'ref')), may hold values from 0 to 191, as said below
- counts: int32 [12288], P(('dp', 'ref')), may hold values from 1 to 12
Outputs:
- sums: float32 [192, 16384], P('ref', 'dp')
- totals: float32 [192], P('ref')
- log_evidence: float32 [12288], P(('dp', 'ref'))
The draws below stay inside these ranges and needn't reach their ends.
Inputs may be any that keep to these rules, and one draw needn't show every extreme that they name: Row p of lists holds 12 distinct orientation indices, clustered near one orientation; only its first counts[p] entries are used.
All inputs are finite; a program needn't handle non-finite values.
Results may differ from the reference program's by a relative error of at most 0.0045.
Values may be sent and summed in bfloat16 or wider, within the bound.
No kernel may reach another device: no remote copies, remote signals or barrier semaphores. Data moves between devices by JAX's collectives and lax.ppermute only.
A program may use at most 128 MiB of HBM per device.

```python
import math
import jax
import jax.numpy as jnp
from jax import lax

GRID = 128
PIX = 8192
TRANS = 9
PARTICLES = 12288
REFS = 192
LIST = 12


def helper_refs(key):
    key = jax.random.fold_in(key, 11)
    return jax.random.normal(key, (REFS, 2 * PIX), jnp.float32)


def helper_ctf(key):
    key = jax.random.fold_in(key, 12)
    return jax.random.uniform(key, (PARTICLES, PIX), jnp.float32, -1.0, 1.0)


def helper_shifts(key):
    key = jax.random.fold_in(key, 13)
    values = jax.random.randint(key, (TRANS, 2), -3, 4, dtype=jnp.int32)
    values = values.at[0].set(jnp.array([3, -3], dtype=jnp.int32))
    return values.at[1].set(jnp.array([-3, 3], dtype=jnp.int32))


def helper_lists(key):
    key = jax.random.fold_in(key, 14)
    first, second = jax.random.split(key)
    window = min(2 * LIST, REFS)
    centre = jax.random.randint(first, (PARTICLES,), 0, REFS, dtype=jnp.int32)
    noise = jax.random.randint(second, (PARTICLES, window), 0, 2 ** 20, dtype=jnp.int32)
    ranked = noise * window + jnp.arange(window, dtype=jnp.int32)[None, :]
    order = jnp.argsort(ranked, axis=1)[:, :LIST].astype(jnp.int32)
    result = (centre[:, None] + order - window // 2) % REFS
    edge = (jnp.arange(LIST, dtype=jnp.int32) - LIST // 2) % REFS
    return result.at[0].set(edge)


def draw_refs(key, part):
    return helper_refs(key).astype(jnp.bfloat16)


def draw_ctf(key, part):
    return helper_ctf(key).astype(jnp.bfloat16)


def draw_shifts(key, part):
    return helper_shifts(key)


def draw_lists(key, part):
    return helper_lists(key)


def draw_counts(key, part):
    key = jax.random.fold_in(key, 5)
    values = jax.random.randint(key, (PARTICLES,), 1, LIST + 1, dtype=jnp.int32)
    values = values.at[0].set(LIST)
    return values.at[1].set(1)


def draw_images(key, part):
    own = jax.random.fold_in(key, 6)
    values = jax.random.normal(own, (PARTICLES, 2 * PIX), jnp.float32)
    return values.astype(jnp.bfloat16)


def setup_inputs(seed: int = 0) -> dict:
    key_list = jax.random.split(jax.random.key(seed), 7)
    return {
        "images": draw_images(jax.random.fold_in(key_list[6], 71), 0),
        "ctf": draw_ctf(jax.random.fold_in(key_list[6], 71), 0),
        "refs": draw_refs(jax.random.fold_in(key_list[6], 71), 0),
        "shifts": draw_shifts(jax.random.fold_in(key_list[6], 71), 0),
        "lists": draw_lists(jax.random.fold_in(key_list[6], 71), 0),
        "counts": draw_counts(jax.random.fold_in(key_list[6], 71), 0),
    }


def phase_tables(shifts):
    half = GRID // 2
    pixel = jnp.arange(PIX, dtype=jnp.int32)
    row = pixel // half
    column = pixel % half
    freq_y = (row + half) % GRID - half
    turns = (column[None, :] * shifts[:, 0:1] + freq_y[None, :] * shifts[:, 1:2]) % GRID
    angle = turns.astype(jnp.float32) * jnp.float32(2.0 * math.pi / GRID)
    return jnp.cos(angle), jnp.sin(angle)


def weighted_rows(image_rows, ctf_rows):
    gain = ctf_rows.astype(jnp.float32)
    real_part = gain * image_rows[:, :PIX].astype(jnp.float32)
    imag_part = gain * image_rows[:, PIX:].astype(jnp.float32)
    return jnp.concatenate([real_part, imag_part], axis=1).astype(jnp.bfloat16)


def reference(images, ctf, refs, shifts, lists, counts):
    cosine, sine = phase_tables(shifts)
    ref_re = refs[:, None, :PIX].astype(jnp.float32)
    ref_im = refs[:, None, PIX:].astype(jnp.float32)
    rot_re = ref_re * cosine[None] - ref_im * sine[None]
    rot_im = ref_re * sine[None] + ref_im * cosine[None]
    rotated = jnp.concatenate([rot_re, rot_im], axis=2).astype(jnp.bfloat16)
    rotated = rotated.reshape(REFS * TRANS, 2 * PIX).astype(jnp.float32)
    scale = jnp.float32((2 * PIX) ** -0.5)
    block = math.gcd(PARTICLES, 2048)
    nblock = PARTICLES // block
    image_blocks = images.reshape(nblock, block, 2 * PIX)
    ctf_blocks = ctf.reshape(nblock, block, PIX)

    def score_block(pair):
        rows = weighted_rows(pair[0], pair[1]).astype(jnp.float32)
        return jnp.dot(rows, rotated.T, preferred_element_type=jnp.float32) * scale

    scores = lax.map(score_block, (image_blocks, ctf_blocks)).reshape(PARTICLES, REFS, TRANS)
    valid = jnp.arange(LIST, dtype=jnp.int32)[None, :] < counts[:, None]
    hits = (lists[:, :, None] == jnp.arange(REFS, dtype=jnp.int32)[None, None, :]) & valid[:, :, None]
    listed = jnp.any(hits, axis=1)[:, :, None]
    masked = jnp.where(listed, scores, -jnp.inf)
    top = jnp.max(masked, axis=(1, 2))
    expd = jnp.where(listed, jnp.exp(masked - top[:, None, None]), jnp.float32(0.0))
    log_evidence = top + jnp.log(jnp.sum(expd, axis=(1, 2)))
    weights = jnp.where(listed, jnp.exp(masked - log_evidence[:, None, None]), jnp.float32(0.0))
    totals = jnp.sum(weights, axis=(0, 2))
    rounded = weights.astype(jnp.bfloat16).reshape(nblock, block, REFS * TRANS)

    def gather_block(total, trio):
        rows = weighted_rows(trio[0], trio[1]).astype(jnp.float32)
        part = jnp.dot(trio[2].astype(jnp.float32).T, rows, preferred_element_type=jnp.float32)
        return total + part, None

    start = jnp.zeros((REFS * TRANS, 2 * PIX), jnp.float32)
    gathered, unused = lax.scan(gather_block, start, (image_blocks, ctf_blocks, rounded))
    gathered = gathered.reshape(REFS, TRANS, 2 * PIX)
    gather_re = gathered[:, :, :PIX]
    gather_im = gathered[:, :, PIX:]
    sums_re = jnp.sum(gather_re * cosine[None] + gather_im * sine[None], axis=1)
    sums_im = jnp.sum(gather_im * cosine[None] - gather_re * sine[None], axis=1)
    sums = jnp.concatenate([sums_re, sums_im], axis=1)
    return sums, totals, log_evidence
```

```python
import math

import jax
import jax.numpy as jnp
from jax import lax
from jax.experimental import pallas as pl
from jax.experimental.pallas import tpu as pltpu
from jax.sharding import Mesh, PartitionSpec as P

GRID = 128
BLOCK = 1024
LANES = 128
GROUPS = BLOCK // LANES
CHUNK = 256
CHIPS = ("z", "y_hi", "y_lo", "x")
EVERYONE = ("y_lo", "x", "core", "z", "y_hi")
SMEM = pl.BlockSpec(memory_space=pltpu.SMEM)
VMEM = pl.BlockSpec(memory_space=pltpu.VMEM)


def pack_kernel(column_ref, odd_ref, refs_ref, out_ref):
    column = pl.multiple_of(column_ref[0] * BLOCK, BLOCK)
    odd = odd_ref[0] == 1
    block = refs_ref[:, pl.ds(column, BLOCK)].astype(jnp.float32)
    whole = jnp.where(odd, block[4:12], block[0:8])
    rest = jnp.where(odd, block[0:4], block[8:12])
    tiles = [whole[:, g * LANES : (g + 1) * LANES] for g in range(GROUPS)]
    tiles += [rest[:, g * LANES : (g + 1) * LANES] for g in range(GROUPS)]
    out_ref[...] = jnp.concatenate(tiles, axis=0).astype(jnp.bfloat16)


def unpack_kernel(odd_ref, flat_ref, out_ref):
    odd = odd_ref[0] == 1
    for g in range(GROUPS):
        lanes = slice(g * LANES, (g + 1) * LANES)
        whole = flat_ref[8 * g : 8 * g + 8]
        rest = flat_ref[8 * GROUPS + 4 * g : 8 * GROUPS + 4 * g + 4]
        block = jnp.where(
            odd,
            jnp.concatenate([rest, whole], axis=0),
            jnp.concatenate([whole, rest], axis=0),
        )
        out_ref[:, lanes] = block


def weighted_kernel(core_ref, images_ref, ctf_ref, own_ref, other_ref):
    core = core_ref[0]
    pairs = own_ref.shape[0] // 2
    for out_ref, half in ((own_ref, core), (other_ref, 1 - core)):
        for pair in range(pairs):
            column = pl.multiple_of((2 * pair + half) * BLOCK, BLOCK)
            gain = ctf_ref[:, pl.ds(column, BLOCK)].astype(jnp.float32)
            for part in range(2):
                start = pl.multiple_of(part * 2 * pairs * BLOCK + column, BLOCK)
                values = images_ref[:, pl.ds(start, BLOCK)].astype(jnp.float32)
                out_ref[part * pairs + pair] = (gain * values).astype(jnp.bfloat16)


def rotate_kernel(core_ref, shifts_ref, own_ref, recv_ref, rot_ref, cos_ref, sin_ref):
    core = core_ref[0]
    pairs, rows = own_ref.shape[0] // 2, own_ref.shape[1]
    trans = shifts_ref.shape[0]
    half = GRID // 2
    steps = BLOCK // CHUNK

    def step(index, carry):
        pair = index // steps
        start = pl.multiple_of((index % steps) * CHUNK, CHUNK)
        lanes = pl.ds(start, CHUNK)
        pixel = (2 * pair + core) * BLOCK + start
        pixel = pixel + lax.broadcasted_iota(jnp.int32, (trans, CHUNK), 1)
        freq_y = (((pixel >> 6) + half) & (GRID - 1)) - half
        turns = (pixel & (half - 1)) * shifts_ref[:, 0:1] + freq_y * shifts_ref[:, 1:2]
        angle = (turns & (GRID - 1)).astype(jnp.float32) * jnp.float32(2.0 * math.pi / GRID)
        cos_ref[...] = jnp.cos(angle)
        sin_ref[...] = jnp.sin(angle)
        for h, half_ref in enumerate((own_ref, recv_ref)):
            re = half_ref[pair, :, lanes].astype(jnp.float32)
            im = half_ref[pairs + pair, :, lanes].astype(jnp.float32)
            for t in range(trans):
                cosine, sine = cos_ref[t : t + 1, :], sin_ref[t : t + 1, :]
                base = (h * trans + t) * rows
                rot_ref[pair, base : base + rows, lanes] = (re * cosine + im * sine).astype(
                    jnp.bfloat16
                )
                rot_ref[pairs + pair, base : base + rows, lanes] = (im * cosine - re * sine).astype(
                    jnp.bfloat16
                )
        return carry

    lax.fori_loop(0, pairs * steps, step, 0)


def spread_piece(flat_ref, wide_ref, piece):
    low = lax.broadcasted_iota(jnp.int32, (8, LANES), 0) < 4
    for two in range(flat_ref.shape[0] // 2):
        even = flat_ref[2 * two, piece].astype(jnp.float32)
        odd = flat_ref[2 * two + 1, piece].astype(jnp.float32)
        row = 24 * two
        for g in range(GROUPS):
            lanes = slice(g * LANES, (g + 1) * LANES)
            wide_ref[row : row + 8, lanes] = even[8 * g : 8 * g + 8]
            wide_ref[row + 16 : row + 24, lanes] = odd[8 * g : 8 * g + 8]
        for j in range(GROUPS // 2):
            at = 8 * (GROUPS + j)
            a, b = even[at : at + 8], odd[at : at + 8]
            lanes = slice(2 * j * LANES, (2 * j + 1) * LANES)
            wide_ref[row + 8 : row + 16, lanes] = jnp.where(low, a, pltpu.roll(b, 4, 0))
            lanes = slice((2 * j + 1) * LANES, (2 * j + 2) * LANES)
            wide_ref[row + 8 : row + 16, lanes] = jnp.where(low, pltpu.roll(a, 4, 0), b)
    return wide_ref[...].astype(jnp.bfloat16)


def forward_kernel(flat_ref, rot_ref, out_ref, wide_ref):
    pairs = rot_ref.shape[0] // 2
    for pair in range(pairs):
        total = None
        for part in range(2):
            piece = part * pairs + pair
            product = lax.dot_general(
                rot_ref[piece],
                spread_piece(flat_ref, wide_ref.at[part], piece),
                (((1,), (1,)), ((), ())),
                preferred_element_type=jnp.float32,
            )
            total = product if total is None else total + product
        count = total.shape[1]
        if pair == 0:
            out_ref[:, :count] = total
            out_ref[:, count:] = jnp.zeros((total.shape[0], out_ref.shape[1] - count), jnp.float32)
        else:
            out_ref[:, :count] += total


def softmax(scale, mine_ref, theirs_ref, lists_ref, weights_ref, evidence_ref, totals_ref):
    particles, slots = lists_ref.shape[1:]
    refs_all = weights_ref.shape[1]
    trans = mine_ref.shape[0] // (2 * particles)
    index = lax.broadcasted_iota(jnp.int32, (particles, refs_all), 1)
    for h in range(2):
        listed = index == lists_ref[h, :, 0:1]
        for k in range(1, slots):
            listed = listed | (index == lists_ref[h, :, k : k + 1])
        scores = []
        for t in range(trans):
            a = (h * trans + t) * particles
            b = ((1 - h) * trans + t) * particles
            value = mine_ref[a : a + particles, :refs_all] + theirs_ref[b : b + particles, :refs_all]
            scores.append(jnp.where(listed, value * scale, -jnp.inf))
        top = scores[0]
        for value in scores[1:]:
            top = jnp.maximum(top, value)
        top = jnp.max(top, axis=1, keepdims=True)
        exps = [jnp.exp(value - top) for value in scores]
        norm = exps[0]
        for value in exps[1:]:
            norm = norm + value
        summed = jnp.sum(norm, axis=1, keepdims=True)
        inverse = 1.0 / summed
        for t in range(trans):
            a = (h * trans + t) * particles
            weights_ref[a : a + particles] = exps[t] * inverse
        if h == 0:
            evidence_ref[...] = top + jnp.log(summed)
            totals_ref[...] = jnp.sum(norm * inverse, axis=0, keepdims=True)


def backward_kernel(
    scale,
    mine_ref,
    theirs_ref,
    lists_ref,
    rot_ref,
    out_ref,
    evidence_ref,
    totals_ref,
    weights_ref,
    flat_ref,
    sems,
):
    softmax(scale, mine_ref, theirs_ref, lists_ref, weights_ref, evidence_ref, totals_ref)
    flipped = weights_ref[...].T.astype(jnp.bfloat16)
    low = lax.broadcasted_iota(jnp.int32, (8, LANES), 0) < 4
    copies = []
    for piece in range(rot_ref.shape[0]):
        product = lax.dot_general(
            flipped, rot_ref[piece], (((1,), (0,)), ((), ())), preferred_element_type=jnp.float32
        )
        for two in range(flat_ref.shape[1] // 2):
            row = 24 * two
            for g in range(GROUPS):
                lanes = slice(g * LANES, (g + 1) * LANES)
                flat_ref[piece, 2 * two, 8 * g : 8 * g + 8] = product[row : row + 8, lanes]
                flat_ref[piece, 2 * two + 1, 8 * g : 8 * g + 8] = product[row + 16 : row + 24, lanes]
            for j in range(GROUPS // 2):
                at = 8 * (GROUPS + j)
                a = product[row + 8 : row + 16, 2 * j * LANES : (2 * j + 1) * LANES]
                b = product[row + 8 : row + 16, (2 * j + 1) * LANES : (2 * j + 2) * LANES]
                flat_ref[piece, 2 * two, at : at + 8] = jnp.where(low, a, pltpu.roll(b, 4, 0))
                flat_ref[piece, 2 * two + 1, at : at + 8] = jnp.where(low, pltpu.roll(a, 4, 0), b)
        copy = pltpu.make_async_copy(flat_ref.at[piece], out_ref.at[:, piece], sems.at[piece])
        copy.start()
        copies.append(copy)
    for copy in copies:
        copy.wait()


def everyones_sum(value):
    for axis in ("core", "y_lo", "y_hi", "x", "z"):
        count = lax.axis_size(axis)
        bit = 1
        while bit < count:
            value = value + lax.ppermute(value, axis, [(i, i ^ bit) for i in range(count)])
            bit *= 2
    return value


def params(mebibytes):
    return pltpu.CompilerParams(vmem_limit_bytes=mebibytes * 1024 * 1024)


def local(images, ctf, refs, shifts, lists, counts):
    parts = images.shape[0]
    rdev = refs.shape[0]
    trans = shifts.shape[0]
    nref = lax.axis_size("z") * lax.axis_size("y_hi")
    pieces = lax.axis_size("y_lo") * lax.axis_size("x")
    refs_all = rdev * nref
    rows = 2 * trans * parts
    swap = [(0, 1), (1, 0)]
    core = lax.axis_index("core")
    column = jnp.full((1,), lax.axis_index(("y_lo", "x")) * 2 + core, jnp.int32)
    odd = jnp.full((1,), lax.axis_index("y_hi"), jnp.int32)
    core = jnp.full((1,), core, jnp.int32)

    mine = pl.pallas_call(
        pack_kernel,
        out_shape=jax.ShapeDtypeStruct((rdev * GROUPS, LANES), jnp.bfloat16),
        in_specs=[SMEM, SMEM, VMEM],
        out_specs=VMEM,
        name="pack",
    )(column, odd, refs)
    gathered = lax.all_gather(mine, CHIPS, axis=0, tiled=True)
    gathered = gathered.reshape(nref, pieces, rdev * GROUPS, LANES)

    half = jax.ShapeDtypeStruct((pieces, parts, BLOCK), jnp.bfloat16)
    own, other = pl.pallas_call(
        weighted_kernel,
        out_shape=(half, half),
        in_specs=[SMEM, VMEM, VMEM],
        out_specs=(VMEM, VMEM),
        compiler_params=params(16),
        name="weighted",
    )(core, images, ctf)
    recv = lax.ppermute(other, "core", swap)
    slot = jnp.arange(lists.shape[1], dtype=jnp.int32)[None, :]
    used = jnp.where(slot < counts[:, None], lists, -1)
    used_pair = jnp.stack([used, lax.ppermute(used, "core", swap)])

    rot = pl.pallas_call(
        rotate_kernel,
        out_shape=jax.ShapeDtypeStruct((pieces, rows, BLOCK), jnp.bfloat16),
        in_specs=[SMEM, VMEM, VMEM, VMEM],
        out_specs=VMEM,
        scratch_shapes=[pltpu.VMEM((trans, CHUNK), jnp.float32)] * 2,
        compiler_params=params(16),
        name="rotate",
    )(core, shifts, own, recv)

    scores = pl.pallas_call(
        forward_kernel,
        out_shape=jax.ShapeDtypeStruct((rows, -(-refs_all // LANES) * LANES), jnp.float32),
        in_specs=[VMEM, VMEM],
        out_specs=VMEM,
        scratch_shapes=[pltpu.VMEM((2, refs_all, BLOCK), jnp.float32)],
        compiler_params=params(16),
        name="forward",
    )(gathered, rot)
    theirs = lax.ppermute(scores, "core", swap)

    scale = (2 * ctf.shape[1]) ** -0.5
    partial, evidence, totals = pl.pallas_call(
        lambda *args: backward_kernel(scale, *args),
        out_shape=(
            jax.ShapeDtypeStruct((nref, pieces, rdev * GROUPS, LANES), jnp.float32),
            jax.ShapeDtypeStruct((parts, 1), jnp.float32),
            jax.ShapeDtypeStruct((1, refs_all), jnp.float32),
        ),
        in_specs=[VMEM, VMEM, VMEM, VMEM],
        out_specs=(pl.BlockSpec(memory_space=pl.ANY), VMEM, VMEM),
        scratch_shapes=[
            pltpu.VMEM((rows, refs_all), jnp.float32),
            pltpu.VMEM((pieces, nref, rdev * GROUPS, LANES), jnp.float32),
            pltpu.SemaphoreType.DMA((pieces,)),
        ],
        compiler_params=params(20),
        name="backward",
    )(scores, theirs, used_pair, rot)

    partial = partial.reshape(nref * pieces * rdev * GROUPS, LANES)
    flat = lax.psum_scatter(partial, CHIPS, scatter_dimension=0, tiled=True)
    sums = pl.pallas_call(
        unpack_kernel,
        out_shape=jax.ShapeDtypeStruct((rdev, BLOCK), jnp.float32),
        in_specs=[SMEM, VMEM],
        out_specs=VMEM,
        name="unpack",
    )(odd, flat)
    all_totals = everyones_sum(totals)[0]
    ref = lax.axis_index(("z", "y_hi"))
    my_totals = lax.dynamic_slice_in_dim(all_totals, ref * rdev, rdev, 0)
    return (sums, my_totals, evidence[:, 0])


def solution(mesh):
    fine = Mesh(mesh.devices.reshape(2, 4, 2, 8, 2), EVERYONE)
    placed = (
        P(EVERYONE, None),
        P(EVERYONE, None),
        P(("z", "y_hi"), None),
        P(),
        P(EVERYONE, None),
        P(EVERYONE),
    )
    return jax.shard_map(
        local,
        mesh=fine,
        in_specs=placed,
        out_specs=(P(("z", "y_hi"), ("y_lo", "x", "core")), P(("z", "y_hi")), P(EVERYONE)),
        check_vma=False,
    )
```

```python
import math

import jax
import jax.numpy as jnp
from jax import lax
from jax.experimental import pallas as pl
from jax.experimental.pallas import tpu as pltpu
from jax.sharding import Mesh, PartitionSpec as P

GRID = 128
BLOCK = 1024
LANES = 128
GROUPS = 4
HALF = 48
CHUNK = 256
EVERYONE = ("y_lo", "x", "core", "z", "y_hi")
SMEM = pl.BlockSpec(memory_space=pltpu.SMEM)
VMEM = pl.BlockSpec(memory_space=pltpu.VMEM)
ANY = pl.BlockSpec(memory_space=pl.ANY)


def over_x(value, bits):
    return lax.ppermute(value, "x", [(i, i ^ bits) for i in range(4)])


def over_y(value, bits):
    bits = {1: 2, 2: 1, 3: 3}[bits]
    return lax.ppermute(value, ("y_lo", "y_hi"), [(i, i ^ bits) for i in range(4)])


def over_z(value, steps):
    return lax.ppermute(value, "z", [(i, (i + steps) % 8) for i in range(8)])


def pack_kernel(column_ref, refs_ref, out_ref):
    column = pl.multiple_of(column_ref[0] * BLOCK, BLOCK)
    block = refs_ref[:, pl.ds(column, BLOCK)].astype(jnp.float32)
    tiles = []
    for side in range(2):
        groups = range(side * GROUPS, (side + 1) * GROUPS)
        tiles += [block[0:8, g * LANES : (g + 1) * LANES] for g in groups]
        tiles += [block[8:12, g * LANES : (g + 1) * LANES] for g in groups]
    out_ref[...] = jnp.concatenate(tiles, axis=0).astype(jnp.bfloat16)


def split_kernel(*args):
    blocks, (p_ref, q_ref) = args[:-2], args[-2:]
    for k, block_ref in enumerate(blocks):
        p_ref[k] = block_ref[:HALF]
        q_ref[k] = block_ref[HALF:]


def join_kernel(*args):
    parts, outs = args[:8], args[8:]
    for n, out_ref in enumerate(outs):
        out_ref[0] = parts[2 * n][...]
        out_ref[1] = parts[2 * n + 1][...]


def weighted_kernel(core_ref, x_ref, images_ref, ctf_ref, packed_ref, own_ref, other_ref):
    core, x = core_ref[0], x_ref[0]
    for out_ref, half in ((own_ref, core), (other_ref, 1 - core)):
        for xr in range(4):
            column = pl.multiple_of((2 * (x ^ xr) + half) * BLOCK, BLOCK)
            gain = ctf_ref[:, pl.ds(column, BLOCK)].astype(jnp.float32)
            for part in range(2):
                start = pl.multiple_of(part * 8 * BLOCK + column, BLOCK)
                values = images_ref[:, pl.ds(start, BLOCK)].astype(jnp.float32)
                out_ref[part, xr] = (gain * values).astype(jnp.bfloat16)


def rotate_kernel(
    core_ref, x_ref, part_ref, shifts_ref, own_ref, recv_ref, rot_ref, cos_ref, sin_ref
):
    rows = own_ref.shape[2]
    trans = shifts_ref.shape[0]
    half = GRID // 2
    first = part_ref[0]
    block = (2 * (x_ref[0] ^ pl.program_id(0)) + core_ref[0]) * BLOCK

    def step(index, carry):
        start = pl.multiple_of(index * CHUNK, CHUNK)
        lanes = pl.ds(start, CHUNK)
        pixel = block + start + lax.broadcasted_iota(jnp.int32, (trans, CHUNK), 1)
        freq_y = (((pixel >> 6) + half) & (GRID - 1)) - half
        turns = (pixel & (half - 1)) * shifts_ref[:, 0:1] + freq_y * shifts_ref[:, 1:2]
        angle = (turns & (GRID - 1)).astype(jnp.float32) * jnp.float32(2.0 * math.pi / GRID)
        cos_ref[...] = jnp.cos(angle)
        sin_ref[...] = jnp.sin(angle)
        for h, half_ref in enumerate((own_ref, recv_ref)):
            re = half_ref[0, 0, :, lanes].astype(jnp.float32)
            im = half_ref[1, 0, :, lanes].astype(jnp.float32)
            for t in range(trans):
                cosine, sine = cos_ref[t : t + 1, :], sin_ref[t : t + 1, :]
                base = (h * trans + t) * rows
                rot_ref[first, 0, base : base + rows, lanes] = (re * cosine + im * sine).astype(
                    jnp.bfloat16
                )
                rot_ref[1 - first, 0, base : base + rows, lanes] = (
                    im * cosine - re * sine
                ).astype(jnp.bfloat16)
        return carry

    lax.fori_loop(0, BLOCK // CHUNK, step, 0)


def low_rows():
    return lax.broadcasted_iota(jnp.int32, (8, LANES), 0) < 4


def spread(own, other, wide_ref, row, column):
    low = low_rows()
    for g in range(GROUPS):
        lanes = slice(column + g * LANES, column + (g + 1) * LANES)
        wide_ref[row : row + 8, lanes] = own[8 * g : 8 * g + 8]
        wide_ref[row + 8 : row + 16, lanes] = other[8 * g : 8 * g + 8]
    for j in range(GROUPS // 2):
        at = 8 * (GROUPS + j)
        a, b = own[at : at + 8], other[at : at + 8]
        start = column + 2 * j * LANES
        wide_ref[row + 16 : row + 24, start : start + LANES] = jnp.where(low, a, pltpu.roll(b, 4, 0))
        start = start + LANES
        wide_ref[row + 16 : row + 24, start : start + LANES] = jnp.where(low, pltpu.roll(a, 4, 0), b)


def gather_up(product, row, column):
    low = low_rows()
    own, other = [], []
    for g in range(GROUPS):
        lanes = slice(column + g * LANES, column + (g + 1) * LANES)
        own.append(product[row : row + 8, lanes])
        other.append(product[row + 8 : row + 16, lanes])
    for j in range(GROUPS // 2):
        start = column + 2 * j * LANES
        a = product[row + 16 : row + 24, start : start + LANES]
        b = product[row + 16 : row + 24, start + LANES : start + 2 * LANES]
        own.append(jnp.where(low, a, pltpu.roll(b, 4, 0)))
        other.append(jnp.where(low, pltpu.roll(a, 4, 0), b))
    return jnp.concatenate(own, axis=0), jnp.concatenate(other, axis=0)


def fetch_all(far_ref, near_ref, sems):
    copies = []
    for b in range(2):
        for xr in range(4):
            copies.append(
                pltpu.make_async_copy(far_ref.at[b, xr], near_ref.at[b, xr], sems.at[b, xr])
            )
            copies[-1].start()
    return copies


def forward_kernel(*args):
    p_refs, q_refs, (far_ref, out_ref, rot_ref, wide_ref, sems) = args[:8], args[8:16], args[16:]
    copies = fetch_all(far_ref, rot_ref, sems)
    for b in range(2):
        for xr in range(4):
            wide = wide_ref.at[xr % 2]
            for k in range(8):
                p = [p_refs[2 * xr + a][b, k].astype(jnp.float32) for a in range(2)]
                q = [
                    q_refs[2 * (2 * a + b) + xr // 2][xr % 2, k].astype(jnp.float32)
                    for a in range(2)
                ]
                spread(p[0], p[1], wide, 24 * k, 0)
                spread(q[0], q[1], wide, 24 * k, BLOCK // 2)
            copies[4 * b + xr].wait()
            product = lax.dot_general(
                rot_ref[b, xr],
                wide[...].astype(jnp.bfloat16),
                (((1,), (1,)), ((), ())),
                preferred_element_type=jnp.float32,
            )
            count = product.shape[1]
            if b == 0 and xr == 0:
                out_ref[:, :count] = product
                out_ref[:, count:] = jnp.zeros(
                    (product.shape[0], out_ref.shape[1] - count), jnp.float32
                )
            else:
                out_ref[:, :count] += product


def orientation(position, z, y_hi):
    k = jnp.zeros_like(position)
    for step in range(1, 8):
        k = k + (position >= 24 * step).astype(jnp.int32)
    place = position - 24 * k
    tail = (place >= 16).astype(jnp.int32)
    late = place - 16 * tail
    a = jnp.where(tail == 1, (late >= 4).astype(jnp.int32), (late >= 8).astype(jnp.int32))
    row = jnp.where(tail == 1, 8 + late - 4 * a, late - 8 * a)
    return (((z - k) & 7) * 2 + (y_hi ^ a)) * 12 + row


def softmax(scale, z, y_hi, mine_ref, theirs_ref, lists_ref, weights_ref, evidence_ref):
    particles, slots = lists_ref.shape[1:]
    refs_all = weights_ref.shape[1]
    trans = mine_ref.shape[0] // (2 * particles)
    shares = []
    index = orientation(lax.broadcasted_iota(jnp.int32, (8, refs_all), 1), z, y_hi)
    index = jnp.concatenate([index] * (particles // 8), axis=0)
    for h in range(2):
        listed = index == lists_ref[h, :, 0:1]
        for slot in range(1, slots):
            listed = listed | (index == lists_ref[h, :, slot : slot + 1])
        scores = []
        for t in range(trans):
            a = (h * trans + t) * particles
            b = ((1 - h) * trans + t) * particles
            value = mine_ref[a : a + particles, :refs_all] + theirs_ref[b : b + particles, :refs_all]
            scores.append(jnp.where(listed, value * scale, -jnp.inf))
        top = scores[0]
        for value in scores[1:]:
            top = jnp.maximum(top, value)
        top = jnp.max(top, axis=1, keepdims=True)
        exps = [jnp.exp(value - top) for value in scores]
        norm = exps[0]
        for value in exps[1:]:
            norm = norm + value
        summed = jnp.sum(norm, axis=1, keepdims=True)
        inverse = 1.0 / summed
        for t in range(trans):
            a = (h * trans + t) * particles
            weights_ref[a : a + particles] = exps[t] * inverse
        if h == 0:
            evidence_ref[...] = top + jnp.log(summed)
        shares.append(jnp.sum(norm * inverse, axis=0, keepdims=True))
    weights_ref[2 * trans * particles :] = jnp.broadcast_to(shares[0] + shares[1], (8, refs_all))


def backward_kernel(scale, z_ref, y_hi_ref, mine_ref, theirs_ref, lists_ref, far_ref, *rest):
    outs, (evidence_ref, totals_ref, weights_ref, rot_ref, sems) = rest[:14], rest[14:]
    copies = fetch_all(far_ref, rot_ref, sems)
    z, y_hi = z_ref[0], y_hi_ref[0]
    softmax(scale, z, y_hi, mine_ref, theirs_ref, lists_ref, weights_ref, evidence_ref)
    flipped = weights_ref[...].T
    refs_all, rows = flipped.shape[0], flipped.shape[1] - 8
    totals = flipped[:, rows : rows + 1]
    index = orientation(lax.broadcasted_iota(jnp.int32, (refs_all, 1), 0), z, y_hi)
    column = lax.broadcasted_iota(jnp.int32, (refs_all, refs_all), 1)
    totals_ref[...] = jnp.sum(jnp.where(index == column, totals, 0.0), axis=0, keepdims=True)
    flipped = flipped[:, :rows].astype(jnp.bfloat16)

    def put(refs, distance, place, k, block):
        stays, far_low, far_high, one_low, one_high, three_low, three_high = refs
        if distance == 0:
            stays[place, k] = block
            return
        low, high = {2: (far_low, far_high), 1: (one_low, one_high), 3: (three_low, three_high)}[
            distance
        ]
        ref = low if k < 4 else high
        ref[place, k % 4] = block.astype(ref.dtype)

    for b in range(2):
        for xr in range(4):
            copies[4 * b + xr].wait()
            product = lax.dot_general(
                flipped, rot_ref[b, xr], (((1,), (0,)), ((), ())), preferred_element_type=jnp.float32
            )
            for k in range(8):
                for a, block in enumerate(gather_up(product, 24 * k, 0)):
                    put(outs[:7], xr, 2 * a + b, k, block)
                for a, block in enumerate(gather_up(product, 24 * k, BLOCK // 2)):
                    put(outs[7:], 2 * a + b, xr, k, block)


def add_totals(refs, out_ref):
    out_ref[...] = (refs[0][...] + refs[1][...]) + (refs[2][...] + refs[3][...])


def add_kernel(*args):
    add_totals(args[:4], args[-1])
    ins, outs = args[4:12], args[12:-1]
    for n, out_ref in enumerate(outs):
        total = ins[2 * n][...] + ins[2 * n + 1][...].astype(jnp.float32)
        out_ref[...] = total.astype(jnp.bfloat16)


def middle_kernel(*args):
    add_totals(args[:4], args[-1])
    ins, outs = args[4:14], args[14:-1]
    for side in range(2):
        stays, one_low, one_high, three_low, three_high = ins[5 * side : 5 * side + 5]
        for n, out_ref in enumerate(outs[4 * side : 4 * side + 4]):
            for ks, one, three in ((0, one_low, three_low), (4, one_high, three_high)):
                total = stays[n, ks : ks + 4] + one[n].astype(jnp.float32)
                total = total + three[n].astype(jnp.float32)
                out_ref[ks : ks + 4] = total.astype(out_ref.dtype)


def late_kernel(*args):
    args[-1][...] = args[0][...] + args[1][...]
    ins, outs = args[2:10], args[10:-1]
    for side in range(2):
        stays, one, two, three = ins[4 * side : 4 * side + 4]
        for k, out_ref in enumerate(outs):
            total = stays[k] + one[k].astype(jnp.float32)
            total = total + (two[k].astype(jnp.float32) + three[k].astype(jnp.float32))
            out_ref[side * HALF : (side + 1) * HALF] = total


def last_kernel(*args):
    add_totals(args[:4], args[-1])
    ins, out_ref = args[4:-2], args[-2]
    total = ins[0][...]
    for ref in ins[1:]:
        total = total + ref[...]
    for side in range(2):
        for g in range(GROUPS):
            start = (side * GROUPS + g) * LANES
            at = side * HALF + 8 * g
            out_ref[0:8, start : start + LANES] = total[at : at + 8]
            at = side * HALF + 8 * GROUPS + 4 * g
            out_ref[8:12, start : start + LANES] = total[at : at + 4]


def across_z(value, bits):
    return lax.ppermute(value, "z", [(i, i ^ bits) for i in range(8)])


def call(name, kernel, ins, outs, specs=None, scratch=(), mebibytes=16):
    single = not isinstance(outs, (list, tuple))
    return pl.pallas_call(
        kernel,
        out_shape=outs,
        in_specs=specs or [VMEM] * len(ins),
        out_specs=VMEM if single else [VMEM] * len(outs),
        scratch_shapes=list(scratch),
        compiler_params=pltpu.CompilerParams(vmem_limit_bytes=mebibytes * 1024 * 1024),
        name=name,
    )(*ins)


def shape(*dims, dtype=jnp.bfloat16):
    return jax.ShapeDtypeStruct(dims, dtype)


def scalar(value):
    return jnp.full((1,), value, jnp.int32)


def local(images, ctf, refs, shifts, lists, counts):
    f32, bf16 = jnp.float32, jnp.bfloat16
    parts, rdev, trans = images.shape[0], refs.shape[0], shifts.shape[0]
    refs_all = rdev * 16
    rows = 2 * trans * parts
    swap = [(0, 1), (1, 0)]
    core, x, y_lo = lax.axis_index("core"), lax.axis_index("x"), lax.axis_index("y_lo")
    z, y_hi = scalar(lax.axis_index("z")), scalar(lax.axis_index("y_hi"))
    column = scalar((y_lo * 4 + x) * 2 + core)
    core, x, y_lo = scalar(core), scalar(x), scalar(y_lo)

    mine = call("pack", pack_kernel, [column, refs], shape(2 * HALF, LANES), [SMEM, VMEM])
    blocks = [mine] + [over_z(mine, k) for k in range(1, 8)]
    p, q = call("split", split_kernel, blocks, [shape(8, HALF, LANES)] * 2)
    ps = [p] + [over_y(p, m) for m in (1, 2, 3)]
    qs = [q] + [over_x(q, m) for m in (1, 2, 3)]
    joined = call("join", join_kernel, ps + qs, [shape(2, 8, HALF, LANES)] * 4)

    def ring(halves, over):
        one0, three1 = over(halves[0], 1), over(halves[1], 3)
        one1, three0 = over(halves[1], 1), over(halves[0], 3)
        two0, two1 = over(one0, 3), over(three1, 1)
        return [*halves, one0, one1, two0, two1, three0, three1]

    p_all = ring(joined[:2], over_x)
    q_all = ring(joined[2:], over_y)

    half = shape(2, 4, parts, BLOCK)
    own, other = call(
        "weighted",
        weighted_kernel,
        [core, x, images, ctf, mine],
        [half, half],
        [SMEM, SMEM, VMEM, VMEM, ANY],
    )
    recv = lax.ppermute(other, "core", swap)
    slot = jnp.arange(lists.shape[1], dtype=jnp.int32)[None, :]
    used = jnp.where(slot < counts[:, None], lists, -1)
    used_pair = jnp.stack([used, lax.ppermute(used, "core", swap)])

    piece = pl.BlockSpec((2, 1, parts, BLOCK), lambda i: (0, i, 0, 0))
    rot = pl.pallas_call(
        rotate_kernel,
        grid=(4,),
        out_shape=shape(2, 4, rows, BLOCK),
        in_specs=[SMEM, SMEM, SMEM, pl.BlockSpec((trans, 2), lambda i: (0, 0)), piece, piece],
        out_specs=pl.BlockSpec((2, 1, rows, BLOCK), lambda i: (0, i, 0, 0)),
        scratch_shapes=[pltpu.VMEM((trans, CHUNK), f32)] * 2,
        compiler_params=pltpu.CompilerParams(vmem_limit_bytes=16 * 1024 * 1024),
        name="rotate",
    )(core, x, y_lo, shifts, own, recv)

    near = [pltpu.VMEM((2, 4, rows, BLOCK), bf16)]
    sems = [pltpu.SemaphoreType.DMA((2, 4))]
    lanes = -(-refs_all // LANES) * LANES
    scores = call(
        "forward",
        forward_kernel,
        p_all + q_all + [rot],
        shape(rows, lanes, dtype=f32),
        [VMEM] * 16 + [ANY],
        near + [pltpu.VMEM((2, refs_all, BLOCK), f32)] + sems,
        26,
    )
    theirs = lax.ppermute(scores, "core", swap)

    scale = (2 * ctf.shape[1]) ** -0.5
    whole = shape(4, 8, HALF, LANES, dtype=f32)
    part16, part32 = shape(4, 4, HALF, LANES), shape(4, 4, HALF, LANES, dtype=f32)
    side = [whole, part16, part16, part16, part32, part32, part16]
    row = shape(1, refs_all, dtype=f32)
    *sums, evidence, totals = call(
        "backward",
        lambda *args: backward_kernel(scale, *args),
        [z, y_hi, scores, theirs, used_pair, rot],
        side * 2 + [shape(parts, 1, dtype=f32), row],
        [SMEM, SMEM, VMEM, VMEM, VMEM, ANY],
        [pltpu.VMEM((rows + 8, refs_all), f32)] + near + sems,
        26,
    )
    first = []
    for over, (_, far_low, far_high, *_) in ((over_x, sums[:7]), (over_y, sums[7:])):
        first.append((over(far_low, 1), over(far_high, 3)))
    ready = []
    for over, (_, _, _, one_low, _, _, three_high) in ((over_x, sums[:7]), (over_y, sums[7:])):
        ready.append((over(one_low, 1), over(three_high, 3)))
    more = call(
        "add",
        add_kernel,
        [totals]
        + [over_y(totals, m) for m in (1, 2, 3)]
        + [sums[4], first[0][1], sums[5], first[0][0]]
        + [sums[11], first[1][1], sums[12], first[1][0]],
        [part16] * 4 + [row],
    )
    totals = more[4]
    ins = []
    for n, over in ((0, over_x), (1, over_y)):
        one_high, three_low = over(more[2 * n], 1), over(more[2 * n + 1], 3)
        ins += [sums[7 * n], ready[n][0], one_high, three_low, ready[n][1]]
    eight16, eight32 = shape(8, HALF, LANES), shape(8, HALF, LANES, dtype=f32)
    ins = [totals] + [over_x(totals, m) for m in (1, 2, 3)] + ins
    middle = call("middle", middle_kernel, ins, [eight32, eight16, eight16, eight16] * 2 + [row])
    totals = middle[8]
    ins = [totals, across_z(totals, 1), middle[0]] + [over_y(middle[m], m) for m in (1, 2, 3)]
    ins += [middle[4]] + [over_x(middle[4 + m], m) for m in (1, 2, 3)]
    late = call("late", late_kernel, ins, [shape(2 * HALF, LANES, dtype=f32)] * 8 + [row])
    ins = [late[8]] + [across_z(late[8], m) for m in (2, 4, 6)]
    ins += [late[0]] + [over_z(late[k], -k) for k in range(1, 8)]
    result, totals = call("last", last_kernel, ins, [shape(rdev, BLOCK, dtype=f32), row])
    ref = lax.axis_index(("z", "y_hi"))
    my_totals = lax.dynamic_slice_in_dim(totals[0], ref * rdev, rdev, 0)
    return (result, my_totals, evidence[:, 0])


def solution(mesh):
    fine = Mesh(mesh.devices.reshape(2, 4, 2, 8, 2), EVERYONE)
    placed = (
        P(EVERYONE, None),
        P(EVERYONE, None),
        P(("z", "y_hi"), None),
        P(),
        P(EVERYONE, None),
        P(EVERYONE),
    )
    return jax.shard_map(
        local,
        mesh=fine,
        in_specs=placed,
        out_specs=(P(("z", "y_hi"), ("y_lo", "x", "core")), P(("z", "y_hi")), P(EVERYONE)),
        check_vma=False,
    )
```

```python
import math

import jax
import jax.numpy as jnp
from jax import lax
from jax.experimental import pallas as pl
from jax.experimental.pallas import tpu as pltpu
from jax.sharding import Mesh, PartitionSpec as P

GRID = 128
BLOCK = 1024
SIDE = BLOCK // 2
LANES = 128
GROUPS = SIDE // LANES
HALF = 48
CHUNK = 256
STACKED = (0, 4, 2, 6, 1, 5, 3, 7)
CHIPS = ("z", "y_hi", "y_lo", "x")
EVERYONE = ("y_lo", "x", "core", "z", "y_hi")
SMEM = pl.BlockSpec(memory_space=pltpu.SMEM)
VMEM = pl.BlockSpec(memory_space=pltpu.VMEM)
ANY = pl.BlockSpec(memory_space=pl.ANY)


def over_z(value, bits):
    return lax.ppermute(value, "z", [(i, i ^ bits) for i in range(8)])


def over(value, bits, core_on_x):
    pairs = []
    for y_lo in range(2):
        for x in range(4):
            for core in range(2):
                for y_hi in range(2):
                    here = ((y_lo * 4 + x) * 2 + core) * 2 + y_hi
                    if core == core_on_x:
                        there = ((y_lo * 4 + (x ^ bits)) * 2 + core) * 2 + y_hi
                    else:
                        there = (((y_lo ^ (bits & 1)) * 4 + x) * 2 + core) * 2 + (y_hi ^ (bits >> 1))
                    pairs.append((here, there))
    return lax.ppermute(value, ("y_lo", "x", "core", "y_hi"), pairs)


def pack_kernel(column_ref, core_ref, refs_ref, out_ref):
    for p in range(2):
        start = pl.multiple_of((2 * column_ref[0] + p) * BLOCK + core_ref[0] * SIDE, SIDE)
        block = refs_ref[:, pl.ds(start, SIDE)].astype(jnp.float32)
        tiles = [block[0:8, g * LANES : (g + 1) * LANES] for g in range(GROUPS)]
        tiles += [block[8:12, g * LANES : (g + 1) * LANES] for g in range(GROUPS)]
        out_ref[0, p] = jnp.concatenate(tiles, axis=0).astype(jnp.bfloat16)


def stack_kernel(*args):
    out_ref = args[-1]
    row = 0
    for ref in args[:-1]:
        count = ref.shape[0]
        out_ref[row : row + count] = ref[...]
        row += count


def join_kernel(own_ref, one_ref, two_ref, three_ref, rot_ref, low_ref, high_ref):
    low_ref[0] = own_ref[...]
    low_ref[1] = one_ref[...]
    high_ref[0] = two_ref[...]
    high_ref[1] = three_ref[...]


def weighted_kernel(core_ref, x_ref, images_ref, ctf_ref, packed_ref, own_ref, other_ref):
    core, x = core_ref[0], x_ref[0]
    for out_ref, side in ((own_ref, core), (other_ref, 1 - core)):
        for xr in range(4):
            for p in range(2):
                column = pl.multiple_of((2 * (x ^ xr) + p) * BLOCK + side * SIDE, SIDE)
                gain = ctf_ref[:, pl.ds(column, SIDE)].astype(jnp.float32)
                for part in range(2):
                    start = pl.multiple_of(part * 8 * BLOCK + column, SIDE)
                    values = images_ref[:, pl.ds(start, SIDE)].astype(jnp.float32)
                    out_ref[part, xr, :, p * SIDE : (p + 1) * SIDE] = (gain * values).astype(
                        jnp.bfloat16
                    )


def rotate_chunk(core, x, shifts_ref, own_ref, recv_ref, xr, start, tables, put):
    rows = own_ref.shape[2]
    trans = shifts_ref.shape[0]
    half = GRID // 2
    cos_ref, sin_ref = tables
    lanes = pl.ds(start, CHUNK)
    pixel = (2 * (x ^ xr) + start // SIDE) * BLOCK + core * SIDE + start % SIDE
    pixel = pixel + lax.broadcasted_iota(jnp.int32, (trans, CHUNK), 1)
    freq_y = (((pixel >> 6) + half) & (GRID - 1)) - half
    turns = (pixel & (half - 1)) * shifts_ref[:, 0:1] + freq_y * shifts_ref[:, 1:2]
    angle = (turns & (GRID - 1)).astype(jnp.float32) * jnp.float32(2.0 * math.pi / GRID)
    cos_ref[...] = jnp.cos(angle)
    sin_ref[...] = jnp.sin(angle)
    for h, half_ref in enumerate((own_ref, recv_ref)):
        re = half_ref[0, xr, :, lanes].astype(jnp.float32)
        im = half_ref[1, xr, :, lanes].astype(jnp.float32)
        for t in range(trans):
            cosine, sine = cos_ref[t : t + 1, :], sin_ref[t : t + 1, :]
            base = (h * trans + t) * rows
            put(0, base, rows, (re * cosine + im * sine).astype(jnp.bfloat16))
            put(1, base, rows, (im * cosine - re * sine).astype(jnp.bfloat16))


def rotate_kernel(
    core_ref, x_ref, part_ref, shifts_ref, own_ref, recv_ref, rot_ref, cos_ref, sin_ref
):
    first = part_ref[0]
    steps = BLOCK // CHUNK

    def step(index, carry):
        xr = index // steps
        start = pl.multiple_of((index % steps) * CHUNK, CHUNK)

        def put(part, base, rows, value):
            rot_ref[part ^ first, xr, base : base + rows, pl.ds(start, CHUNK)] = value

        rotate_chunk(
            core_ref[0], x_ref[0], shifts_ref, own_ref, recv_ref, xr, start, (cos_ref, sin_ref), put
        )
        return carry

    lax.fori_loop(0, 4 * steps, step, 0)


def low_rows():
    return lax.broadcasted_iota(jnp.int32, (8, LANES), 0) < 4


def spread(own, other, wide_ref, row, column):
    low = low_rows()
    for g in range(GROUPS):
        lanes = slice(column + g * LANES, column + (g + 1) * LANES)
        wide_ref[row : row + 8, lanes] = own[8 * g : 8 * g + 8]
        wide_ref[row + 8 : row + 16, lanes] = other[8 * g : 8 * g + 8]
    for j in range(GROUPS // 2):
        at = 8 * (GROUPS + j)
        a, b = own[at : at + 8], other[at : at + 8]
        start = column + 2 * j * LANES
        wide_ref[row + 16 : row + 24, start : start + LANES] = jnp.where(low, a, pltpu.roll(b, 4, 0))
        start = start + LANES
        wide_ref[row + 16 : row + 24, start : start + LANES] = jnp.where(low, pltpu.roll(a, 4, 0), b)


def forward_kernel(*args):
    core_ref, blocks, (rot_ref, out_ref, wide_ref) = args[0], args[1:9], args[9:]
    first = core_ref[0] == 0

    def block(n, m, k):
        return blocks[2 * n + m // 2][m % 2, STACKED[k]].astype(jnp.float32)

    for b in range(2):
        for xr in range(4):
            wide = wide_ref.at[xr % 2]
            for k in range(8):
                pair = []
                for a in range(2):
                    y = 2 * a + b
                    value = block(xr, y, k)
                    if y != xr:
                        value = jnp.where(first, value, block(y, xr, k))
                    pair.append(value)
                for p in range(2):
                    spread(pair[0][p], pair[1][p], wide, 24 * k, p * SIDE)
            product = lax.dot_general(
                rot_ref[b, xr],
                wide[...].astype(jnp.bfloat16),
                (((1,), (1,)), ((), ())),
                preferred_element_type=jnp.float32,
            )
            count = product.shape[1]
            if b == 0 and xr == 0:
                out_ref[:, :count] = product
                out_ref[:, count:] = jnp.zeros(
                    (product.shape[0], out_ref.shape[1] - count), jnp.float32
                )
            else:
                out_ref[:, :count] += product


def orientation(position, z, y_hi):
    k = jnp.zeros_like(position)
    for step in range(1, 8):
        k = k + (position >= 24 * step).astype(jnp.int32)
    place = position - 24 * k
    tail = (place >= 16).astype(jnp.int32)
    late = place - 16 * tail
    a = jnp.where(tail == 1, (late >= 4).astype(jnp.int32), (late >= 8).astype(jnp.int32))
    row = jnp.where(tail == 1, 8 + late - 4 * a, late - 8 * a)
    return ((z ^ k) * 2 + (y_hi ^ a)) * 12 + row


def softmax(scale, z, y_hi, mine_ref, theirs_ref, lists_ref, weights_ref, evidence_ref):
    particles, slots = lists_ref.shape[1:]
    refs_all = weights_ref.shape[1]
    trans = mine_ref.shape[0] // (2 * particles)
    shares = []
    index = orientation(lax.broadcasted_iota(jnp.int32, (8, refs_all), 1), z, y_hi)
    index = jnp.concatenate([index] * (particles // 8), axis=0)
    for h in range(2):
        listed = index == lists_ref[h, :, 0:1]
        for slot in range(1, slots):
            listed = listed | (index == lists_ref[h, :, slot : slot + 1])
        scores = []
        for t in range(trans):
            a = (h * trans + t) * particles
            b = ((1 - h) * trans + t) * particles
            value = mine_ref[a : a + particles, :refs_all] + theirs_ref[b : b + particles, :refs_all]
            scores.append(jnp.where(listed, value * scale, -jnp.inf))
        top = scores[0]
        for value in scores[1:]:
            top = jnp.maximum(top, value)
        top = jnp.max(top, axis=1, keepdims=True)
        exps = [jnp.exp(value - top) for value in scores]
        norm = exps[0]
        for value in exps[1:]:
            norm = norm + value
        summed = jnp.sum(norm, axis=1, keepdims=True)
        inverse = 1.0 / summed
        for t in range(trans):
            a = (h * trans + t) * particles
            weights_ref[a : a + particles] = exps[t] * inverse
        if h == 0:
            evidence_ref[...] = top + jnp.log(summed)
        shares.append(jnp.sum(norm * inverse, axis=0, keepdims=True))
    weights_ref[2 * trans * particles :] = jnp.broadcast_to(shares[0] + shares[1], (8, refs_all))


def backward_kernel(scale, *args):
    core_ref, x_ref, y_lo_ref, z_ref, y_hi_ref, mine_ref, theirs_ref, lists_ref = args[:8]
    shifts_ref, own_ref, recv_ref = args[8:11]
    stays, far_low, far_high, one_low, one_high, three_low, three_high = args[11:18]
    evidence_ref, totals_ref, weights_ref, rot_ref, sums_ref, cos_ref, sin_ref = args[18:]
    core, x, y_lo, z, y_hi = core_ref[0], x_ref[0], y_lo_ref[0], z_ref[0], y_hi_ref[0]
    softmax(scale, z, y_hi, mine_ref, theirs_ref, lists_ref, weights_ref, evidence_ref)
    flipped = weights_ref[...].T
    refs_all, rows = flipped.shape[0], flipped.shape[1] - 8
    index = orientation(lax.broadcasted_iota(jnp.int32, (refs_all, 1), 0), z, y_hi)
    column = lax.broadcasted_iota(jnp.int32, (refs_all, refs_all), 1)
    totals = jnp.where(index == column, flipped[:, rows : rows + 1], 0.0)
    totals = jnp.sum(totals, axis=0, keepdims=True)
    totals_ref[...] = jnp.zeros(totals_ref.shape, jnp.float32)
    totals_ref[0:1, :] = totals[:, :LANES]
    totals_ref[1:2, : refs_all - LANES] = totals[:, LANES:]
    weights = flipped[:, :rows].astype(jnp.bfloat16)
    low = low_rows()

    def step(at, carry):
        xr, p = at // 2, at % 2
        for c in range(SIDE // CHUNK):
            start = pl.multiple_of(p * SIDE + c * CHUNK, CHUNK)

            def put(part, base, rows, value):
                rot_ref[c, part, base : base + rows, :] = value

            tables = cos_ref.at[c], sin_ref.at[c]
            rotate_chunk(core, x, shifts_ref, own_ref, recv_ref, xr, start, tables, put)
            for part in range(2):
                product = lax.dot_general(
                    weights,
                    rot_ref[c, part],
                    (((1,), (0,)), ((), ())),
                    preferred_element_type=jnp.float32,
                )
                for a in range(2):
                    y = 2 * a + (part ^ y_lo)
                    i, j = jnp.where(core == 0, xr, y), jnp.where(core == 0, y, xr)
                    for k in range(8):
                        row = 24 * k
                        ref = sums_ref.at[i, j, k, p]
                        for g in range(2):
                            to = 8 * (2 * c + g)
                            ref[to : to + 8] = product[
                                row + 8 * a : row + 8 * a + 8, g * LANES : (g + 1) * LANES
                            ]
                        one = product[row + 16 : row + 24, :LANES]
                        two = product[row + 16 : row + 24, LANES:]
                        if a == 0:
                            tail = jnp.where(low, one, pltpu.roll(two, 4, 0))
                        else:
                            tail = jnp.where(low, pltpu.roll(one, 4, 0), two)
                        to = 8 * (GROUPS + c)
                        ref[to : to + 8] = tail
        return carry

    lax.fori_loop(0, 8, step, 0)
    for place in range(4):
        stays[place] = sums_ref[0, place]
        for distance, low_ref, high_ref in (
            (2, far_low, far_high),
            (1, one_low, one_high),
            (3, three_low, three_high),
        ):
            low_ref[place] = sums_ref[distance, place, 0:4].astype(low_ref.dtype)
            high_ref[place] = sums_ref[distance, place, 4:8].astype(high_ref.dtype)


def add_kernel(one_ref, one_more_ref, three_ref, three_more_ref, one_out, three_out):
    one_out[...] = (one_ref[...] + one_more_ref[...].astype(jnp.float32)).astype(jnp.bfloat16)
    three_out[...] = (three_ref[...] + three_more_ref[...].astype(jnp.float32)).astype(jnp.bfloat16)


def middle_kernel(stays, one_low, one_high, three_low, three_high, *outs):
    for n, out_ref in enumerate(outs):
        for ks, one, three in ((0, one_low, three_low), (4, one_high, three_high)):
            total = stays[n, ks : ks + 4] + one[n].astype(jnp.float32)
            total = total + three[n].astype(jnp.float32)
            out_ref[ks : ks + 4] = total.astype(out_ref.dtype)


def late_kernel(stays, one, two, three, even_ref, odd_ref):
    for k in range(8):
        total = stays[k] + one[k].astype(jnp.float32)
        total = total + (two[k].astype(jnp.float32) + three[k].astype(jnp.float32))
        if k % 2 == 0:
            even_ref[k // 2] = total
        else:
            odd_ref[k // 2] = total.astype(odd_ref.dtype)


def halve_kernel(stays, came, even_ref, odd_ref):
    for k in range(stays.shape[0]):
        total = stays[k] + came[k].astype(jnp.float32)
        if k % 2 == 0:
            even_ref[k // 2] = total
        else:
            odd_ref[k // 2] = total


def deal_kernel(core_ref, stays, came, mine_ref, give_ref):
    first = core_ref[0] == 0
    low, high = stays[0, 0] + came[0, 0], stays[0, 1] + came[0, 1]
    mine_ref[...] = jnp.where(first, low, high)
    give_ref[...] = jnp.where(first, high, low)


def last_kernel(core_ref, mine_ref, came_ref, out_ref):
    first = core_ref[0] == 0
    low = jnp.where(first, mine_ref[...], came_ref[...])
    high = jnp.where(first, came_ref[...], mine_ref[...])
    for side, block in enumerate((low, high)):
        for g in range(GROUPS):
            start = side * SIDE + g * LANES
            out_ref[0:8, start : start + LANES] = block[8 * g : 8 * g + 8]
            at = 8 * GROUPS + 4 * g
            out_ref[8:12, start : start + LANES] = block[at : at + 4]


def totals_kernel(ref_ref, all_ref, out_ref):
    total = jnp.sum(all_ref[...], axis=0)
    row = jnp.concatenate([total[0:1], total[1:2]], axis=1)
    row = jnp.broadcast_to(row, (8, 2 * LANES))
    row = pltpu.roll(row, (2 * LANES - 12 * ref_ref[0]) % (2 * LANES), 1)
    out_ref[...] = row[0:1, :LANES]


def call(name, kernel, ins, outs, specs=None, scratch=(), mebibytes=16, micros=1):
    single = not isinstance(outs, (list, tuple))
    return pl.pallas_call(
        kernel,
        out_shape=outs,
        in_specs=specs or [VMEM] * len(ins),
        out_specs=VMEM if single else [VMEM] * len(outs),
        scratch_shapes=list(scratch),
        compiler_params=pltpu.CompilerParams(vmem_limit_bytes=mebibytes * 1024 * 1024),
        cost_estimate=pl.CostEstimate(
            flops=micros * 1000000, bytes_accessed=micros * 3000000, transcendentals=0
        ),
        name=name,
    )(*ins)


def shape(*dims, dtype=jnp.bfloat16):
    return jax.ShapeDtypeStruct(dims, dtype)


def scalar(value):
    return jnp.full((1,), value, jnp.int32)


def local(images, ctf, refs, shifts, lists, counts):
    f32, bf16 = jnp.float32, jnp.bfloat16
    parts, rdev, trans = images.shape[0], refs.shape[0], shifts.shape[0]
    refs_all = rdev * 16
    rows = 2 * trans * parts
    swap = [(0, 1), (1, 0)]
    core, x, y_lo = lax.axis_index("core"), lax.axis_index("x"), lax.axis_index("y_lo")
    z, y_hi = scalar(lax.axis_index("z")), scalar(lax.axis_index("y_hi"))
    ref = scalar(lax.axis_index(("z", "y_hi")))
    column = scalar(y_lo * 4 + x)
    core, x, y_lo = scalar(core), scalar(x), scalar(y_lo)

    mine = call(
        "pack", pack_kernel, [column, core, refs], shape(1, 2, HALF, LANES), [SMEM, SMEM, VMEM]
    )
    half = shape(2, 4, parts, BLOCK)
    own, other = call(
        "weighted",
        weighted_kernel,
        [core, x, images, ctf, mine],
        [half, half],
        [SMEM, SMEM, VMEM, VMEM, ANY],
    )
    recv = lax.ppermute(other, "core", swap)
    slot = jnp.arange(lists.shape[1], dtype=jnp.int32)[None, :]
    used = jnp.where(slot < counts[:, None], lists, -1)
    used_pair = jnp.stack([used, lax.ppermute(used, "core", swap)])
    tables = [pltpu.VMEM((trans, CHUNK), f32)] * 2
    rot = call(
        "rotate",
        rotate_kernel,
        [core, x, y_lo, shifts, own, recv],
        shape(2, 4, rows, BLOCK),
        [SMEM] * 3 + [VMEM] * 3,
        tables,
        8,
        6,
    )

    blocks = mine
    for bits in (4, 2, 1):
        came = over_z(blocks, bits)
        blocks = call(
            "stack", stack_kernel, [blocks, came], shape(2 * blocks.shape[0], 2, HALF, LANES)
        )
    fours = [blocks] + [over(blocks, m, 1) for m in (1, 2, 3)]
    low, high = call(
        "join", join_kernel, fours + [rot], [shape(2, 8, 2, HALF, LANES)] * 2, [VMEM] * 4 + [ANY]
    )
    one_low, three_high = over(low, 1, 0), over(high, 3, 0)
    one_high, three_low = over(high, 1, 0), over(low, 3, 0)
    two_low, two_high = over(one_low, 3, 0), over(three_high, 1, 0)
    lanes = -(-refs_all // LANES) * LANES
    scores = call(
        "forward",
        forward_kernel,
        [core, low, high, one_low, one_high, two_low, two_high, three_low, three_high, rot],
        shape(rows, lanes, dtype=f32),
        [SMEM] + [VMEM] * 9,
        [pltpu.VMEM((2, refs_all, BLOCK), f32)],
        16,
        4,
    )
    theirs = lax.ppermute(scores, "core", swap)

    scale = (2 * ctf.shape[1]) ** -0.5
    part16, part32 = shape(4, 4, 2, HALF, LANES), shape(4, 4, 2, HALF, LANES, dtype=f32)
    stays, far_low, far_high, one_low, one_high, three_low, three_high, evidence, totals = call(
        "backward",
        lambda *args: backward_kernel(scale, *args),
        [core, x, y_lo, z, y_hi, scores, theirs, used_pair, shifts, own, recv],
        [shape(4, 8, 2, HALF, LANES, dtype=f32), part16, part16, part16, part32, part32, part16]
        + [shape(parts, 1, dtype=f32), shape(8, LANES, dtype=f32)],
        [SMEM] * 5 + [VMEM] * 6,
        [
            pltpu.VMEM((rows + 8, refs_all), f32),
            pltpu.VMEM((2, 2, rows, CHUNK), bf16),
            pltpu.VMEM((4, 4, 8, 2, HALF, LANES), f32),
            pltpu.VMEM((2, trans, CHUNK), f32),
            pltpu.VMEM((2, trans, CHUNK), f32),
        ],
        24,
        10,
    )
    all_totals = lax.all_gather(totals, CHIPS, axis=0, tiled=False)
    far_one, far_three = over(far_low, 1, 0), over(far_high, 3, 0)
    one_low, three_high = over(one_low, 1, 0), over(three_high, 3, 0)
    one_high, three_low = call(
        "add", add_kernel, [one_high, far_three, three_low, far_one], [part16, part16]
    )
    one_high, three_low = over(one_high, 1, 0), over(three_low, 3, 0)
    eight16, eight32 = shape(8, 2, HALF, LANES), shape(8, 2, HALF, LANES, dtype=f32)
    middle = call(
        "middle",
        middle_kernel,
        [stays, one_low, one_high, three_low, three_high],
        [eight32, eight16, eight16, eight16],
    )
    came = [over(middle[m], m, 1) for m in (1, 2, 3)]
    even, odd = call(
        "late",
        late_kernel,
        [middle[0]] + came,
        [shape(4, 2, HALF, LANES, dtype=f32), shape(4, 2, HALF, LANES)],
    )
    came = over_z(odd, 1)
    two32 = shape(2, 2, HALF, LANES, dtype=f32)
    even, odd = call("halve", halve_kernel, [even, came], [two32, two32])
    came = over_z(odd, 2)
    one32 = shape(1, 2, HALF, LANES, dtype=f32)
    even, odd = call("halve", halve_kernel, [even, came], [one32, one32])
    came = over_z(odd, 4)
    block = shape(HALF, LANES, dtype=f32)
    mine, give = call("deal", deal_kernel, [core, even, came], [block, block], [SMEM, VMEM, VMEM])
    came = lax.ppermute(give, "core", swap)
    result = call(
        "last",
        last_kernel,
        [core, mine, came],
        shape(rdev, BLOCK, dtype=f32),
        [SMEM, VMEM, VMEM],
    )
    my_totals = call(
        "totals", totals_kernel, [ref, all_totals], shape(1, LANES, dtype=f32), [SMEM, VMEM]
    )
    return (result, my_totals[0, :rdev], evidence[:, 0])


def solution(mesh):
    fine = Mesh(mesh.devices.reshape(2, 4, 2, 8, 2), EVERYONE)
    placed = (
        P(EVERYONE, None),
        P(EVERYONE, None),
        P(("z", "y_hi"), None),
        P(),
        P(EVERYONE, None),
        P(EVERYONE),
    )
    return jax.shard_map(
        local,
        mesh=fine,
        in_specs=placed,
        out_specs=(P(("z", "y_hi"), ("y_lo", "x", "core")), P(("z", "y_hi")), P(EVERYONE)),
        check_vma=False,
    )
```

```python
import functools
import math

import jax
import jax.numpy as jnp
from jax import lax
from jax.experimental import pallas as pl
from jax.experimental.pallas import tpu as pltpu
from jax.sharding import Mesh, PartitionSpec as P

GRID = 128
BLOCK = 1024
SIDE = BLOCK // 2
LANES = 128
GROUPS = SIDE // LANES
HALF = 48
CHUNK = 256
STACKED = (0, 4, 2, 6, 1, 5, 3, 7)
EVERYONE = ("y_lo", "x", "core", "z", "y_hi")
SMEM = pl.BlockSpec(memory_space=pltpu.SMEM)
VMEM = pl.BlockSpec(memory_space=pltpu.VMEM)
ANY = pl.BlockSpec(memory_space=pl.ANY)


def over_z(value, bits):
    return lax.ppermute(value, "z", [(i, i ^ bits) for i in range(8)])


def over(value, bits, core_on_x):
    pairs = []
    for y_lo in range(2):
        for x in range(4):
            for core in range(2):
                for y_hi in range(2):
                    here = ((y_lo * 4 + x) * 2 + core) * 2 + y_hi
                    if core == core_on_x:
                        there = ((y_lo * 4 + (x ^ bits)) * 2 + core) * 2 + y_hi
                    else:
                        there = (((y_lo ^ (bits & 1)) * 4 + x) * 2 + core) * 2 + (y_hi ^ (bits >> 1))
                    pairs.append((here, there))
    return lax.ppermute(value, ("y_lo", "x", "core", "y_hi"), pairs)


def pack_kernel(column_ref, core_ref, refs_ref, out_ref):
    for p in range(2):
        start = pl.multiple_of((2 * column_ref[0] + p) * BLOCK + core_ref[0] * SIDE, SIDE)
        block = refs_ref[:, pl.ds(start, SIDE)].astype(jnp.float32)
        tiles = [block[0:8, g * LANES : (g + 1) * LANES] for g in range(GROUPS)]
        tiles += [block[8:12, g * LANES : (g + 1) * LANES] for g in range(GROUPS)]
        out_ref[0, p] = jnp.concatenate(tiles, axis=0).astype(jnp.bfloat16)


def stack_kernel(own_ref, came_ref, *rest):
    out_ref = rest[-1]
    count = own_ref.shape[0]
    out_ref[:count] = own_ref[...]
    out_ref[count:] = came_ref[...]


def join_kernel(own_ref, one_ref, two_ref, three_ref, rot_ref, low_ref, high_ref):
    low_ref[0] = own_ref[...]
    low_ref[1] = one_ref[...]
    high_ref[0] = two_ref[...]
    high_ref[1] = three_ref[...]


def weighted_kernel(core_ref, x_ref, images_ref, ctf_ref, packed_ref, own_ref, other_ref):
    core, x = core_ref[0], x_ref[0]
    for out_ref, side in ((own_ref, core), (other_ref, 1 - core)):
        for xr in range(4):
            for p in range(2):
                column = pl.multiple_of((2 * (x ^ xr) + p) * BLOCK + side * SIDE, SIDE)
                gain = ctf_ref[:, pl.ds(column, SIDE)].astype(jnp.float32)
                for part in range(2):
                    start = pl.multiple_of(part * 8 * BLOCK + column, SIDE)
                    values = images_ref[:, pl.ds(start, SIDE)].astype(jnp.float32)
                    out_ref[part, xr, :, p * SIDE : (p + 1) * SIDE] = (gain * values).astype(
                        jnp.bfloat16
                    )


def rotate_chunk(core, x, shifts_ref, own_ref, recv_ref, xr, start, tables, put):
    rows = own_ref.shape[2]
    trans = shifts_ref.shape[0]
    half = GRID // 2
    cos_ref, sin_ref = tables
    lanes = pl.ds(start, CHUNK)
    pixel = (2 * (x ^ xr) + start // SIDE) * BLOCK + core * SIDE + start % SIDE
    pixel = pixel + lax.broadcasted_iota(jnp.int32, (trans, CHUNK), 1)
    freq_y = (((pixel >> 6) + half) & (GRID - 1)) - half
    turns = (pixel & (half - 1)) * shifts_ref[:, 0:1] + freq_y * shifts_ref[:, 1:2]
    angle = (turns & (GRID - 1)).astype(jnp.float32) * jnp.float32(2.0 * math.pi / GRID)
    cos_ref[...] = jnp.cos(angle)
    sin_ref[...] = jnp.sin(angle)
    for h, half_ref in enumerate((own_ref, recv_ref)):
        re = half_ref[0, xr, :, lanes].astype(jnp.float32)
        im = half_ref[1, xr, :, lanes].astype(jnp.float32)
        for t in range(trans):
            cosine, sine = cos_ref[t : t + 1, :], sin_ref[t : t + 1, :]
            base = (h * trans + t) * rows
            put(0, base, rows, (re * cosine + im * sine).astype(jnp.bfloat16))
            put(1, base, rows, (im * cosine - re * sine).astype(jnp.bfloat16))


def rotate_kernel(
    first_xr, core_ref, x_ref, part_ref, shifts_ref, own_ref, recv_ref, rot_ref, cos_ref, sin_ref
):
    first = part_ref[0]
    steps = BLOCK // CHUNK

    def step(index, carry):
        xr = index // steps
        start = pl.multiple_of((index % steps) * CHUNK, CHUNK)

        def put(part, base, rows, value, place=xr):
            rot_ref[part ^ first, place, base : base + rows, pl.ds(start, CHUNK)] = value

        tables = cos_ref, sin_ref
        xr = first_xr + xr
        rotate_chunk(core_ref[0], x_ref[0], shifts_ref, own_ref, recv_ref, xr, start, tables, put)
        return carry

    lax.fori_loop(0, rot_ref.shape[1] * steps, step, 0)


def three_parts(value):
    terms = []
    for _ in range(3):
        term = value.astype(jnp.bfloat16)
        terms.append(term.astype(jnp.float32))
        value = value - terms[-1]
    terms.append(jnp.zeros((HALF - 24, LANES), jnp.float32))
    return jnp.concatenate(terms, axis=0).astype(jnp.bfloat16)


def whole(block):
    block = block.astype(jnp.float32)
    return (block[0:8] + block[8:16]) + block[16:24]


def low_rows():
    return lax.broadcasted_iota(jnp.int32, (8, LANES), 0) < 4


def spread(own, other, wide_ref, row, column):
    low = low_rows()
    for g in range(GROUPS):
        lanes = slice(column + g * LANES, column + (g + 1) * LANES)
        wide_ref[row : row + 8, lanes] = own[8 * g : 8 * g + 8]
        wide_ref[row + 8 : row + 16, lanes] = other[8 * g : 8 * g + 8]
    for j in range(GROUPS // 2):
        at = 8 * (GROUPS + j)
        a, b = own[at : at + 8], other[at : at + 8]
        start = column + 2 * j * LANES
        wide_ref[row + 16 : row + 24, start : start + LANES] = jnp.where(low, a, pltpu.roll(b, 4, 0))
        start = start + LANES
        wide_ref[row + 16 : row + 24, start : start + LANES] = jnp.where(low, pltpu.roll(a, 4, 0), b)


def forward_kernel(*args):
    core_ref, blocks, rots, (out_ref, wide_ref) = args[0], args[1:9], args[9:11], args[11:]
    first = core_ref[0] == 0

    def block(n, m, k):
        return blocks[2 * n + m // 2][m % 2, STACKED[k]].astype(jnp.float32)

    for b in range(2):
        for xr in range(4):
            wide = wide_ref.at[xr % 2]
            for k in range(8):
                pair = []
                for a in range(2):
                    y = 2 * a + b
                    value = block(xr, y, k)
                    if y != xr:
                        value = jnp.where(first, value, block(y, xr, k))
                    pair.append(value)
                for p in range(2):
                    spread(pair[0][p], pair[1][p], wide, 24 * k, p * SIDE)
            product = lax.dot_general(
                rots[xr // 2][b, xr % 2],
                wide[...].astype(jnp.bfloat16),
                (((1,), (1,)), ((), ())),
                preferred_element_type=jnp.float32,
            )
            count = product.shape[1]
            if b == 0 and xr == 0:
                out_ref[:, :count] = product
                out_ref[:, count:] = jnp.zeros(
                    (product.shape[0], out_ref.shape[1] - count), jnp.float32
                )
            else:
                out_ref[:, :count] += product


def orientation(position, z, y_hi):
    k = jnp.zeros_like(position)
    for step in range(1, 8):
        k = k + (position >= 24 * step).astype(jnp.int32)
    place = position - 24 * k
    tail = (place >= 16).astype(jnp.int32)
    late = place - 16 * tail
    a = jnp.where(tail == 1, (late >= 4).astype(jnp.int32), (late >= 8).astype(jnp.int32))
    row = jnp.where(tail == 1, 8 + late - 4 * a, late - 8 * a)
    return ((z ^ k) * 2 + (y_hi ^ a)) * 12 + row


def softmax(scale, z, y_hi, mine_ref, theirs_ref, lists_ref, weights_ref, evidence_ref):
    particles, slots = lists_ref.shape[1:]
    refs_all = weights_ref.shape[1]
    trans = mine_ref.shape[0] // (2 * particles)
    shares = []
    index = orientation(lax.broadcasted_iota(jnp.int32, (8, refs_all), 1), z, y_hi)
    index = jnp.concatenate([index] * (particles // 8), axis=0)
    for h in range(2):
        listed = index == lists_ref[h, :, 0:1]
        for slot in range(1, slots):
            listed = listed | (index == lists_ref[h, :, slot : slot + 1])
        scores = []
        for t in range(trans):
            a = (h * trans + t) * particles
            b = ((1 - h) * trans + t) * particles
            value = mine_ref[a : a + particles, :refs_all] + theirs_ref[b : b + particles, :refs_all]
            scores.append(jnp.where(listed, value * scale, -jnp.inf))
        top = scores[0]
        for value in scores[1:]:
            top = jnp.maximum(top, value)
        top = jnp.max(top, axis=1, keepdims=True)
        exps = [jnp.exp(value - top) for value in scores]
        norm = exps[0]
        for value in exps[1:]:
            norm = norm + value
        summed = jnp.sum(norm, axis=1, keepdims=True)
        inverse = 1.0 / summed
        for t in range(trans):
            a = (h * trans + t) * particles
            weights_ref[a : a + particles] = exps[t] * inverse
        if h == 0:
            evidence_ref[...] = top + jnp.log(summed)
        shares.append(jnp.sum(norm * inverse, axis=0, keepdims=True))
    weights_ref[2 * trans * particles :] = jnp.broadcast_to(shares[0] + shares[1], (8, refs_all))


def backward_kernel(scale, *args):
    core_ref, x_ref, y_lo_ref, z_ref, y_hi_ref, mine_ref, theirs_ref, lists_ref = args[:8]
    shifts_ref, own_ref, recv_ref = args[8:11]
    stays, far_low, far_high, one_low, one_high, three_low, three_high = args[11:18]
    evidence_ref, totals_ref, weights_ref, rot_ref, sums_ref, cos_ref, sin_ref = args[18:]
    core, x, y_lo, z, y_hi = core_ref[0], x_ref[0], y_lo_ref[0], z_ref[0], y_hi_ref[0]
    softmax(scale, z, y_hi, mine_ref, theirs_ref, lists_ref, weights_ref, evidence_ref)
    flipped = weights_ref[...].T
    refs_all, rows = flipped.shape[0], flipped.shape[1] - 8
    index = orientation(lax.broadcasted_iota(jnp.int32, (refs_all, 1), 0), z, y_hi)
    column = lax.broadcasted_iota(jnp.int32, (refs_all, refs_all), 1)
    totals = jnp.where(index == column, flipped[:, rows : rows + 1], 0.0)
    totals = jnp.sum(totals, axis=0, keepdims=True)
    totals_ref[...] = jnp.zeros(totals_ref.shape, jnp.float32)
    totals_ref[0:1, :] = totals[:, :LANES]
    totals_ref[1:2, : refs_all - LANES] = totals[:, LANES:]
    parts = three_parts(totals_ref[...])
    totals_ref[...] = whole(parts)
    far_low[32] = parts
    far_high[32] = parts
    weights = flipped[:, :rows].astype(jnp.bfloat16)
    low = low_rows()

    def step(at, carry):
        xr, p = at // 2, at % 2
        for c in range(SIDE // CHUNK):
            start = pl.multiple_of(p * SIDE + c * CHUNK, CHUNK)

            def put(part, base, rows, value):
                rot_ref[c, part, base : base + rows, :] = value

            tables = cos_ref.at[c], sin_ref.at[c]
            rotate_chunk(core, x, shifts_ref, own_ref, recv_ref, xr, start, tables, put)
            for part in range(2):
                product = lax.dot_general(
                    weights,
                    rot_ref[c, part],
                    (((1,), (0,)), ((), ())),
                    preferred_element_type=jnp.float32,
                )
                for a in range(2):
                    y = 2 * a + (part ^ y_lo)
                    i, j = jnp.where(core == 0, xr, y), jnp.where(core == 0, y, xr)
                    for k in range(8):
                        row = 24 * k
                        ref = sums_ref.at[i, j, k, p]
                        for g in range(2):
                            to = 8 * (2 * c + g)
                            ref[to : to + 8] = product[
                                row + 8 * a : row + 8 * a + 8, g * LANES : (g + 1) * LANES
                            ]
                        one = product[row + 16 : row + 24, :LANES]
                        two = product[row + 16 : row + 24, LANES:]
                        if a == 0:
                            tail = jnp.where(low, one, pltpu.roll(two, 4, 0))
                        else:
                            tail = jnp.where(low, pltpu.roll(one, 4, 0), two)
                        to = 8 * (GROUPS + c)
                        ref[to : to + 8] = tail
        return carry

    lax.fori_loop(0, 8, step, 0)
    for place in range(4):
        stays[place] = sums_ref[0, place]
        for distance, low_ref, high_ref in (
            (2, far_low, far_high),
            (1, one_low, one_high),
            (3, three_low, three_high),
        ):
            for k in range(4):
                for p in range(2):
                    at = 8 * place + 2 * k + p
                    low_ref[at] = sums_ref[distance, place, k, p].astype(low_ref.dtype)
                    high_ref[at] = sums_ref[distance, place, 4 + k, p].astype(high_ref.dtype)


def add_kernel(
    totals_ref, one_ref, far_three, three_ref, far_one, one_out, three_out, both_ref, third_ref
):
    one_out[0:32] = (one_ref[...] + far_three[0:32].astype(jnp.float32)).astype(jnp.bfloat16)
    one_out[32] = far_three[32]
    three_out[...] = (three_ref[...] + far_one[0:32].astype(jnp.float32)).astype(jnp.bfloat16)
    both_ref[...] = totals_ref[...] + whole(far_one[32])
    third_ref[...] = whole(far_three[32])


def middle_kernel(both_ref, third_ref, stays, one_low, one_high, three_low, three_high, *outs):
    totals_ref = outs[-1]
    totals = both_ref[...] + (whole(one_high[32]) + third_ref[...])
    parts = three_parts(totals)
    totals_ref[...] = whole(parts)
    for n, out_ref in enumerate(outs[:-1]):
        if n:
            out_ref[16] = parts
        for ks, one, three in ((0, one_low, three_low), (4, one_high, three_high)):
            for k in range(4):
                for p in range(2):
                    at = 8 * n + 2 * k + p
                    total = stays[n, ks + k, p] + one[at].astype(jnp.float32)
                    total = total + three[at].astype(jnp.float32)
                    out_ref[2 * (ks + k) + p] = total.astype(out_ref.dtype)


def late_kernel(totals_ref, stays, one, two, three, even_ref, odd_ref, sum_ref):
    totals = totals_ref[...] + whole(one[16])
    totals = totals + (whole(two[16]) + whole(three[16]))
    parts = three_parts(totals)
    sum_ref[...] = whole(parts)
    odd_ref[8] = parts
    for k in range(8):
        for p in range(2):
            at = 2 * k + p
            total = stays[at] + one[at].astype(jnp.float32)
            total = total + (two[at].astype(jnp.float32) + three[at].astype(jnp.float32))
            if k % 2 == 0:
                even_ref[2 * (k // 2) + p] = total
            else:
                odd_ref[2 * (k // 2) + p] = total.astype(odd_ref.dtype)


def halve_kernel(totals_ref, stays, came, even_ref, odd_ref, sum_ref):
    count = stays.shape[0] // 2
    last = came[2 * count]
    if last.dtype == jnp.bfloat16:
        totals = totals_ref[...] + whole(last)
    else:
        totals = totals_ref[...] + last[0:8]
    sum_ref[...] = totals
    odd_ref[count] = jnp.zeros((HALF, LANES), jnp.float32)
    odd_ref[count, 0:8] = totals
    for k in range(count):
        for p in range(2):
            total = stays[2 * k + p] + came[2 * k + p].astype(jnp.float32)
            if k % 2 == 0:
                even_ref[2 * (k // 2) + p] = total
            else:
                odd_ref[2 * (k // 2) + p] = total


def deal_kernel(core_ref, totals_ref, stays, came, mine_ref, give_ref):
    first = core_ref[0] == 0
    low, high = stays[0] + came[0], stays[1] + came[1]
    totals = totals_ref[...] + came[2, 0:8]
    mine_ref[0] = jnp.where(first, low, high)
    give_ref[0] = jnp.where(first, high, low)
    for ref in (mine_ref, give_ref):
        ref[1] = jnp.zeros((HALF, LANES), jnp.float32)
        ref[1, 0:8] = totals


def last_kernel(core_ref, ref_ref, mine_ref, came_ref, out_ref, totals_ref):
    first = core_ref[0] == 0
    low = jnp.where(first, mine_ref[0], came_ref[0])
    high = jnp.where(first, came_ref[0], mine_ref[0])
    total = jnp.where(first, mine_ref[1, 0:8], came_ref[1, 0:8])
    row = jnp.concatenate([total[0:1], total[1:2]], axis=1)
    row = jnp.broadcast_to(row, (8, 2 * LANES))
    row = pltpu.roll(row, (2 * LANES - 12 * ref_ref[0]) % (2 * LANES), 1)
    totals_ref[...] = row[0:1, :LANES]
    for side, block in enumerate((low, high)):
        for g in range(GROUPS):
            start = side * SIDE + g * LANES
            out_ref[0:8, start : start + LANES] = block[8 * g : 8 * g + 8]
            at = 8 * GROUPS + 4 * g
            out_ref[8:12, start : start + LANES] = block[at : at + 4]


def call(name, kernel, ins, outs, specs=None, scratch=(), mebibytes=16, micros=1):
    single = not isinstance(outs, (list, tuple))
    return pl.pallas_call(
        kernel,
        out_shape=outs,
        in_specs=specs or [VMEM] * len(ins),
        out_specs=VMEM if single else [VMEM] * len(outs),
        scratch_shapes=list(scratch),
        compiler_params=pltpu.CompilerParams(vmem_limit_bytes=mebibytes * 1024 * 1024),
        cost_estimate=pl.CostEstimate(
            flops=micros * 1000000, bytes_accessed=micros * 3000000, transcendentals=0
        ),
        name=name,
    )(*ins)


def shape(*dims, dtype=jnp.bfloat16):
    return jax.ShapeDtypeStruct(dims, dtype)


def scalar(value):
    return jnp.full((1,), value, jnp.int32)


def local(images, ctf, refs, shifts, lists, counts):
    f32, bf16 = jnp.float32, jnp.bfloat16
    parts, rdev, trans = images.shape[0], refs.shape[0], shifts.shape[0]
    refs_all = rdev * 16
    rows = 2 * trans * parts
    swap = [(0, 1), (1, 0)]
    core, x, y_lo = lax.axis_index("core"), lax.axis_index("x"), lax.axis_index("y_lo")
    z, y_hi = scalar(lax.axis_index("z")), scalar(lax.axis_index("y_hi"))
    ref = scalar(lax.axis_index(("z", "y_hi")))
    column = scalar(y_lo * 4 + x)
    core, x, y_lo = scalar(core), scalar(x), scalar(y_lo)

    mine = call(
        "pack", pack_kernel, [column, core, refs], shape(1, 2, HALF, LANES), [SMEM, SMEM, VMEM]
    )
    four = call(
        "stack", stack_kernel, [mine, over_z(mine, 4)], shape(2, 2, HALF, LANES)
    )
    half = shape(2, 4, parts, BLOCK)
    own, other = call(
        "weighted",
        weighted_kernel,
        [core, x, images, ctf, four],
        [half, half],
        [SMEM, SMEM, VMEM, VMEM, ANY],
    )
    recv = lax.ppermute(other, "core", swap)
    slot = jnp.arange(lists.shape[1], dtype=jnp.int32)[None, :]
    used = jnp.where(slot < counts[:, None], lists, -1)
    used_pair = jnp.stack([used, lax.ppermute(used, "core", swap)])
    tables = [pltpu.VMEM((trans, CHUNK), f32)] * 2
    rots = []
    for first_xr in (0, 2):
        rots.append(
            call(
                "rotate",
                functools.partial(rotate_kernel, first_xr),
                [core, x, y_lo, shifts, own, recv],
                shape(2, 2, rows, BLOCK),
                [SMEM] * 3 + [VMEM] * 3,
                tables,
                8,
                3,
            )
        )
    two = call(
        "stack",
        stack_kernel,
        [four, over_z(four, 2), recv],
        shape(4, 2, HALF, LANES),
        [VMEM, VMEM, ANY],
    )
    blocks = call(
        "stack",
        stack_kernel,
        [two, over_z(two, 1), rots[0]],
        shape(8, 2, HALF, LANES),
        [VMEM, VMEM, ANY],
    )
    fours = [blocks] + [over(blocks, m, 1) for m in (1, 2, 3)]
    low, high = call(
        "join", join_kernel, fours + [rots[1]], [shape(2, 8, 2, HALF, LANES)] * 2, [VMEM] * 4 + [ANY]
    )
    one_low, three_high = over(low, 1, 0), over(high, 3, 0)
    one_high, three_low = over(high, 1, 0), over(low, 3, 0)
    two_low, two_high = over(one_low, 3, 0), over(three_high, 1, 0)
    lanes = -(-refs_all // LANES) * LANES
    scores = call(
        "forward",
        forward_kernel,
        [core, low, high, one_low, one_high, two_low, two_high, three_low, three_high]
        + rots,
        shape(rows, lanes, dtype=f32),
        [SMEM] + [VMEM] * 10,
        [pltpu.VMEM((2, refs_all, BLOCK), f32)],
        16,
        4,
    )
    theirs = lax.ppermute(scores, "core", swap)

    scale = (2 * ctf.shape[1]) ** -0.5
    part16, part32 = shape(32, HALF, LANES), shape(32, HALF, LANES, dtype=f32)
    more16, row = shape(33, HALF, LANES), shape(8, LANES, dtype=f32)
    stays, far_low, far_high, one_low, one_high, three_low, three_high, evidence, totals = call(
        "backward",
        lambda *args: backward_kernel(scale, *args),
        [core, x, y_lo, z, y_hi, scores, theirs, used_pair, shifts, own, recv],
        [shape(4, 8, 2, HALF, LANES, dtype=f32), more16, more16, part16, part32, part32, part16]
        + [shape(parts, 1, dtype=f32), row],
        [SMEM] * 5 + [VMEM] * 6,
        [
            pltpu.VMEM((rows + 8, refs_all), f32),
            pltpu.VMEM((2, 2, rows, CHUNK), bf16),
            pltpu.VMEM((4, 4, 8, 2, HALF, LANES), f32),
            pltpu.VMEM((2, trans, CHUNK), f32),
            pltpu.VMEM((2, trans, CHUNK), f32),
        ],
        24,
        10,
    )
    far_one, far_three = over(far_low, 1, 0), over(far_high, 3, 0)
    one_low, three_high = over(one_low, 1, 0), over(three_high, 3, 0)
    one_high, three_low, both, third = call(
        "add",
        add_kernel,
        [totals, one_high, far_three, three_low, far_one],
        [more16, part16, row, row],
    )
    one_high, three_low = over(one_high, 1, 0), over(three_low, 3, 0)
    *middle, totals = call(
        "middle",
        middle_kernel,
        [both, third, stays, one_low, one_high, three_low, three_high],
        [shape(16, HALF, LANES, dtype=f32)] + [shape(17, HALF, LANES)] * 3 + [row],
    )
    came = [over(middle[m], m, 1) for m in (1, 2, 3)]
    even, odd, totals = call(
        "late",
        late_kernel,
        [totals, middle[0]] + came,
        [shape(8, HALF, LANES, dtype=f32), shape(9, HALF, LANES), row],
    )
    for bits, count in ((1, 4), (2, 2)):
        even, odd, totals = call(
            "halve",
            halve_kernel,
            [totals, even, over_z(odd, bits)],
            [
                shape(count, HALF, LANES, dtype=f32),
                shape(count + 1, HALF, LANES, dtype=f32),
                row,
            ],
        )
    two32 = shape(2, HALF, LANES, dtype=f32)
    mine, give = call(
        "deal", deal_kernel, [core, totals, even, over_z(odd, 4)], [two32, two32], [SMEM] + [VMEM] * 3
    )
    came = lax.ppermute(give, "core", swap)
    result, totals = call(
        "last",
        last_kernel,
        [core, ref, mine, came],
        [shape(rdev, BLOCK, dtype=f32), shape(1, LANES, dtype=f32)],
        [SMEM, SMEM, VMEM, VMEM],
    )
    return (result, totals[0, :rdev], evidence[:, 0])


def solution(mesh):
    fine = Mesh(mesh.devices.reshape(2, 4, 2, 8, 2), EVERYONE)
    placed = (
        P(EVERYONE, None),
        P(EVERYONE, None),
        P(("z", "y_hi"), None),
        P(),
        P(EVERYONE, None),
        P(EVERYONE),
    )
    return jax.shard_map(
        local,
        mesh=fine,
        in_specs=placed,
        out_specs=(P(("z", "y_hi"), ("y_lo", "x", "core")), P(("z", "y_hi")), P(EVERYONE)),
        check_vma=False,
    )
```

```python
import functools
import math

import jax
import jax.numpy as jnp
from jax import lax
from jax.experimental import pallas as pl
from jax.experimental.pallas import tpu as pltpu
from jax.sharding import Mesh, PartitionSpec as P

GRID = 128
BLOCK = 1024
SIDE = BLOCK // 2
LANES = 128
GROUPS = SIDE // LANES
HALF = 48
CHUNK = 256
STACKED = (0, 4, 1, 5, 2, 6, 3, 7)
EVERYONE = ("y_lo", "x", "core", "z", "y_hi")
SMEM = pl.BlockSpec(memory_space=pltpu.SMEM)
VMEM = pl.BlockSpec(memory_space=pltpu.VMEM)
ANY = pl.BlockSpec(memory_space=pl.ANY)


def over_z(value, bits):
    return lax.ppermute(value, "z", [(i, i ^ bits) for i in range(8)])


def over(value, bits, core_on_x):
    pairs = []
    for y_lo in range(2):
        for x in range(4):
            for core in range(2):
                for y_hi in range(2):
                    here = ((y_lo * 4 + x) * 2 + core) * 2 + y_hi
                    if core == core_on_x:
                        there = ((y_lo * 4 + (x ^ bits)) * 2 + core) * 2 + y_hi
                    else:
                        there = (((y_lo ^ (bits & 1)) * 4 + x) * 2 + core) * 2 + (y_hi ^ (bits >> 1))
                    pairs.append((here, there))
    return lax.ppermute(value, ("y_lo", "x", "core", "y_hi"), pairs)


def pack_kernel(column_ref, core_ref, refs_ref, out_ref):
    for p in range(2):
        start = pl.multiple_of((2 * column_ref[0] + p) * BLOCK + core_ref[0] * SIDE, SIDE)
        block = refs_ref[:, pl.ds(start, SIDE)].astype(jnp.float32)
        tiles = [block[0:8, g * LANES : (g + 1) * LANES] for g in range(GROUPS)]
        tiles += [block[8:12, g * LANES : (g + 1) * LANES] for g in range(GROUPS)]
        out_ref[0, p] = jnp.concatenate(tiles, axis=0).astype(jnp.bfloat16)


def stack_kernel(*args):
    row = 0
    for ref in args[:-2]:
        count = ref.shape[0]
        args[-1][row : row + count] = ref[...]
        row += count


def join_kernel(own_ref, one_ref, two_ref, three_ref, rot_ref, low_ref, high_ref):
    low_ref[0] = own_ref[...]
    low_ref[1] = one_ref[...]
    high_ref[0] = two_ref[...]
    high_ref[1] = three_ref[...]


def weighted_kernel(core_ref, x_ref, images_ref, ctf_ref, before_ref, own_ref, other_ref):
    core, x = core_ref[0], x_ref[0]
    for out_ref, side in ((own_ref, core), (other_ref, 1 - core)):
        for xr in range(4):
            for p in range(2):
                column = pl.multiple_of((2 * (x ^ xr) + p) * BLOCK + side * SIDE, SIDE)
                gain = ctf_ref[:, pl.ds(column, SIDE)].astype(jnp.float32)
                for part in range(2):
                    start = pl.multiple_of(part * 8 * BLOCK + column, SIDE)
                    values = images_ref[:, pl.ds(start, SIDE)].astype(jnp.float32)
                    out_ref[part, xr, :, p * SIDE : (p + 1) * SIDE] = (gain * values).astype(
                        jnp.bfloat16
                    )


def rotate_chunk(core, x, shifts_ref, own_ref, recv_ref, xr, start, tables, put):
    rows = own_ref.shape[2]
    trans = shifts_ref.shape[0]
    half = GRID // 2
    cos_ref, sin_ref = tables
    lanes = pl.ds(start, CHUNK)
    pixel = (2 * (x ^ xr) + start // SIDE) * BLOCK + core * SIDE + start % SIDE
    pixel = pixel + lax.broadcasted_iota(jnp.int32, (trans, CHUNK), 1)
    freq_y = (((pixel >> 6) + half) & (GRID - 1)) - half
    turns = (pixel & (half - 1)) * shifts_ref[:, 0:1] + freq_y * shifts_ref[:, 1:2]
    angle = (turns & (GRID - 1)).astype(jnp.float32) * jnp.float32(2.0 * math.pi / GRID)
    cos_ref[...] = jnp.cos(angle)
    sin_ref[...] = jnp.sin(angle)
    for h, half_ref in enumerate((own_ref, recv_ref)):
        re = half_ref[0, xr, :, lanes].astype(jnp.float32)
        im = half_ref[1, xr, :, lanes].astype(jnp.float32)
        for t in range(trans):
            cosine, sine = cos_ref[t : t + 1, :], sin_ref[t : t + 1, :]
            base = (h * trans + t) * rows
            put(0, base, rows, (re * cosine + im * sine).astype(jnp.bfloat16))
            put(1, base, rows, (im * cosine - re * sine).astype(jnp.bfloat16))


def rotate_kernel(
    first_xr, core_ref, x_ref, part_ref, shifts_ref, own_ref, recv_ref, rot_ref, cos_ref, sin_ref
):
    first = part_ref[0]
    steps = BLOCK // CHUNK

    def step(index, carry):
        xr = index // steps
        start = pl.multiple_of((index % steps) * CHUNK, CHUNK)

        def put(part, base, rows, value, place=xr):
            rot_ref[part ^ first, place, base : base + rows, pl.ds(start, CHUNK)] = value

        tables = cos_ref, sin_ref
        xr = first_xr + xr
        rotate_chunk(core_ref[0], x_ref[0], shifts_ref, own_ref, recv_ref, xr, start, tables, put)
        return carry

    lax.fori_loop(0, rot_ref.shape[1] * steps, step, 0)


def three_parts(value):
    terms = []
    for _ in range(3):
        term = value.astype(jnp.bfloat16)
        terms.append(term.astype(jnp.float32))
        value = value - terms[-1]
    terms.append(jnp.zeros((HALF - 24, LANES), jnp.float32))
    return jnp.concatenate(terms, axis=0).astype(jnp.bfloat16)


def whole(block):
    block = block.astype(jnp.float32)
    return (block[0:8] + block[8:16]) + block[16:24]


def low_rows():
    return lax.broadcasted_iota(jnp.int32, (8, LANES), 0) < 4


def spread(own, other, wide_ref, row, column):
    low = low_rows()
    for g in range(GROUPS):
        lanes = slice(column + g * LANES, column + (g + 1) * LANES)
        wide_ref[row : row + 8, lanes] = own[8 * g : 8 * g + 8]
        wide_ref[row + 8 : row + 16, lanes] = other[8 * g : 8 * g + 8]
    for j in range(GROUPS // 2):
        at = 8 * (GROUPS + j)
        a, b = own[at : at + 8], other[at : at + 8]
        start = column + 2 * j * LANES
        wide_ref[row + 16 : row + 24, start : start + LANES] = jnp.where(low, a, pltpu.roll(b, 4, 0))
        start = start + LANES
        wide_ref[row + 16 : row + 24, start : start + LANES] = jnp.where(low, pltpu.roll(a, 4, 0), b)


def forward_kernel(*args):
    core_ref, blocks, rots, (out_ref, wide_ref) = args[0], args[1:9], args[9:11], args[11:]
    first = core_ref[0] == 0

    def block(n, m, k):
        return blocks[2 * n + m // 2][m % 2, STACKED[k]].astype(jnp.float32)

    for b in range(2):
        for xr in range(4):
            wide = wide_ref.at[xr % 2]
            for k in range(8):
                pair = []
                for a in range(2):
                    y = 2 * a + b
                    value = block(xr, y, k)
                    if y != xr:
                        value = jnp.where(first, value, block(y, xr, k))
                    pair.append(value)
                for p in range(2):
                    spread(pair[0][p], pair[1][p], wide, 24 * k, p * SIDE)
            product = lax.dot_general(
                rots[xr // 2][b, xr % 2],
                wide[...].astype(jnp.bfloat16),
                (((1,), (1,)), ((), ())),
                preferred_element_type=jnp.float32,
            )
            count = product.shape[1]
            if b == 0 and xr == 0:
                out_ref[:, :count] = product
                out_ref[:, count:] = jnp.zeros(
                    (product.shape[0], out_ref.shape[1] - count), jnp.float32
                )
            else:
                out_ref[:, :count] += product


def orientation(position, z, y_hi):
    k = jnp.zeros_like(position)
    for step in range(1, 8):
        k = k + (position >= 24 * step).astype(jnp.int32)
    place = position - 24 * k
    tail = (place >= 16).astype(jnp.int32)
    late = place - 16 * tail
    a = jnp.where(tail == 1, (late >= 4).astype(jnp.int32), (late >= 8).astype(jnp.int32))
    row = jnp.where(tail == 1, 8 + late - 4 * a, late - 8 * a)
    return ((z ^ k) * 2 + (y_hi ^ a)) * 12 + row


def softmax(scale, z, y_hi, mine_ref, theirs_ref, lists_ref, weights_ref, evidence_ref):
    particles, slots = lists_ref.shape[1:]
    refs_all = weights_ref.shape[1]
    trans = mine_ref.shape[0] // (2 * particles)
    shares = []
    index = orientation(lax.broadcasted_iota(jnp.int32, (8, refs_all), 1), z, y_hi)
    index = jnp.concatenate([index] * (particles // 8), axis=0)
    for h in range(2):
        listed = index == lists_ref[h, :, 0:1]
        for slot in range(1, slots):
            listed = listed | (index == lists_ref[h, :, slot : slot + 1])
        scores = []
        for t in range(trans):
            a = (h * trans + t) * particles
            b = ((1 - h) * trans + t) * particles
            value = mine_ref[a : a + particles, :refs_all] + theirs_ref[b : b + particles, :refs_all]
            scores.append(jnp.where(listed, value * scale, -jnp.inf))
        top = scores[0]
        for value in scores[1:]:
            top = jnp.maximum(top, value)
        top = jnp.max(top, axis=1, keepdims=True)
        exps = [jnp.exp(value - top) for value in scores]
        norm = exps[0]
        for value in exps[1:]:
            norm = norm + value
        summed = jnp.sum(norm, axis=1, keepdims=True)
        inverse = 1.0 / summed
        for t in range(trans):
            a = (h * trans + t) * particles
            weights_ref[a : a + particles] = exps[t] * inverse
        if h == 0:
            evidence_ref[...] = top + jnp.log(summed)
        shares.append(jnp.sum(norm * inverse, axis=0, keepdims=True))
    weights_ref[2 * trans * particles :] = jnp.broadcast_to(shares[0] + shares[1], (8, refs_all))


def backward_kernel(scale, *args):
    core_ref, x_ref, y_lo_ref, z_ref, y_hi_ref, mine_ref, theirs_ref, lists_ref = args[:8]
    shifts_ref, own_ref, recv_ref = args[8:11]
    stays, to_one, to_three, one_high, three_low = args[11:16]
    evidence_ref, totals_ref, weights_ref, rot_ref, sums_ref, cos_ref, sin_ref = args[16:]
    core, x, y_lo, z, y_hi = core_ref[0], x_ref[0], y_lo_ref[0], z_ref[0], y_hi_ref[0]
    softmax(scale, z, y_hi, mine_ref, theirs_ref, lists_ref, weights_ref, evidence_ref)
    flipped = weights_ref[...].T
    refs_all, rows = flipped.shape[0], flipped.shape[1] - 8
    index = orientation(lax.broadcasted_iota(jnp.int32, (refs_all, 1), 0), z, y_hi)
    column = lax.broadcasted_iota(jnp.int32, (refs_all, refs_all), 1)
    totals = jnp.where(index == column, flipped[:, rows : rows + 1], 0.0)
    totals = jnp.sum(totals, axis=0, keepdims=True)
    totals_ref[...] = jnp.zeros(totals_ref.shape, jnp.float32)
    totals_ref[0:1, :] = totals[:, :LANES]
    totals_ref[1:2, : refs_all - LANES] = totals[:, LANES:]
    parts = three_parts(totals_ref[...])
    totals_ref[...] = whole(parts)
    to_one[64] = parts
    to_three[64] = parts
    weights = flipped[:, :rows].astype(jnp.bfloat16)
    low = low_rows()

    def step(at, carry):
        xr, p = at // 2, at % 2
        for c in range(SIDE // CHUNK):
            start = pl.multiple_of(p * SIDE + c * CHUNK, CHUNK)

            def put(part, base, rows, value):
                rot_ref[c, part, base : base + rows, :] = value

            tables = cos_ref.at[c], sin_ref.at[c]
            rotate_chunk(core, x, shifts_ref, own_ref, recv_ref, xr, start, tables, put)
            for part in range(2):
                product = lax.dot_general(
                    weights,
                    rot_ref[c, part],
                    (((1,), (0,)), ((), ())),
                    preferred_element_type=jnp.float32,
                )
                for a in range(2):
                    y = 2 * a + (part ^ y_lo)
                    i, j = jnp.where(core == 0, xr, y), jnp.where(core == 0, y, xr)
                    for k in range(8):
                        row = 24 * k
                        ref = sums_ref.at[i, j, k, p]
                        for g in range(2):
                            to = 8 * (2 * c + g)
                            ref[to : to + 8] = product[
                                row + 8 * a : row + 8 * a + 8, g * LANES : (g + 1) * LANES
                            ]
                        one = product[row + 16 : row + 24, :LANES]
                        two = product[row + 16 : row + 24, LANES:]
                        if a == 0:
                            tail = jnp.where(low, one, pltpu.roll(two, 4, 0))
                        else:
                            tail = jnp.where(low, pltpu.roll(one, 4, 0), two)
                        to = 8 * (GROUPS + c)
                        ref[to : to + 8] = tail
        return carry

    lax.fori_loop(0, 8, step, 0)
    for place in range(4):
        stays[place] = sums_ref[0, place]
        for distance, low_ref, low_at, high_ref, high_at in (
            (2, to_one, 0, to_three, 0),
            (1, to_one, 32, one_high, 0),
            (3, three_low, 0, to_three, 32),
        ):
            for k in range(4):
                for p in range(2):
                    at = 8 * place + 2 * k + p
                    low = sums_ref[distance, place, k, p]
                    high = sums_ref[distance, place, 4 + k, p]
                    low_ref[low_at + at] = low.astype(low_ref.dtype)
                    high_ref[high_at + at] = high.astype(high_ref.dtype)


def add_kernel(
    totals_ref, one_ref, three_ref, from_one, from_three, one_out, three_out, both_ref, third_ref
):
    one_out[0:32] = (one_ref[...] + from_three[0:32].astype(jnp.float32)).astype(jnp.bfloat16)
    one_out[32] = from_three[64]
    three_out[...] = (three_ref[...] + from_one[0:32].astype(jnp.float32)).astype(jnp.bfloat16)
    both_ref[...] = totals_ref[...] + whole(from_one[64])
    third_ref[...] = whole(from_three[64])


def middle_kernel(both_ref, third_ref, stays, from_one, one_high, three_low, from_three, *outs):
    totals_ref = outs[-1]
    totals = both_ref[...] + (whole(one_high[32]) + third_ref[...])
    parts = three_parts(totals)
    totals_ref[...] = whole(parts)
    for n, out_ref in enumerate(outs[:-1]):
        if n:
            out_ref[16] = parts
        for ks, one, one_at, three, three_at in (
            (0, from_one, 32, three_low, 0),
            (4, one_high, 0, from_three, 32),
        ):
            for k in range(4):
                for p in range(2):
                    at = 8 * n + 2 * k + p
                    total = stays[n, ks + k, p] + one[one_at + at].astype(jnp.float32)
                    total = total + three[three_at + at].astype(jnp.float32)
                    out_ref[2 * (ks + k) + p] = total.astype(out_ref.dtype)


def late_kernel(totals_ref, stays, one, two, three, even_ref, odd_ref, sum_ref):
    totals = totals_ref[...] + whole(one[16])
    totals = totals + (whole(two[16]) + whole(three[16]))
    parts = three_parts(totals)
    sum_ref[...] = whole(parts)
    odd_ref[8] = parts
    for k in range(8):
        for p in range(2):
            at = 2 * k + p
            total = stays[at] + one[at].astype(jnp.float32)
            total = total + (two[at].astype(jnp.float32) + three[at].astype(jnp.float32))
            if k % 2 == 0:
                even_ref[2 * (k // 2) + p] = total
            else:
                odd_ref[2 * (k // 2) + p] = total.astype(odd_ref.dtype)


def halve_kernel(totals_ref, stays, came, own_ref, two_ref, four_ref, six_ref, sum_ref):
    totals = totals_ref[...] + whole(came[8])
    sum_ref[...] = totals
    for k, ref in enumerate((own_ref, two_ref, four_ref, six_ref)):
        for p in range(2):
            ref[p] = stays[2 * k + p] + came[2 * k + p].astype(jnp.float32)
        if k:
            ref[2] = jnp.zeros((HALF, LANES), jnp.float32)
            ref[2, 0:8] = totals


def deal_kernel(core_ref, totals_ref, stays, two, four, six, mine_ref, give_ref):
    first = core_ref[0] == 0
    low, high = [(stays[p] + two[p]) + (four[p] + six[p]) for p in range(2)]
    totals = (totals_ref[...] + two[2, 0:8]) + (four[2, 0:8] + six[2, 0:8])
    mine_ref[0] = jnp.where(first, low, high)
    give_ref[0] = jnp.where(first, high, low)
    for ref in (mine_ref, give_ref):
        ref[1] = jnp.zeros((HALF, LANES), jnp.float32)
        ref[1, 0:8] = totals


def last_kernel(core_ref, ref_ref, mine_ref, came_ref, out_ref, totals_ref):
    first = core_ref[0] == 0
    low = jnp.where(first, mine_ref[0], came_ref[0])
    high = jnp.where(first, came_ref[0], mine_ref[0])
    total = jnp.where(first, mine_ref[1, 0:8], came_ref[1, 0:8])
    row = jnp.concatenate([total[0:1], total[1:2]], axis=1)
    row = jnp.broadcast_to(row, (8, 2 * LANES))
    row = pltpu.roll(row, (2 * LANES - 12 * ref_ref[0]) % (2 * LANES), 1)
    totals_ref[...] = row[0:1, :LANES]
    for side, block in enumerate((low, high)):
        for g in range(GROUPS):
            start = side * SIDE + g * LANES
            out_ref[0:8, start : start + LANES] = block[8 * g : 8 * g + 8]
            at = 8 * GROUPS + 4 * g
            out_ref[8:12, start : start + LANES] = block[at : at + 4]


def call(name, kernel, ins, outs, specs=None, scratch=(), mebibytes=16, micros=1):
    single = not isinstance(outs, (list, tuple))
    return pl.pallas_call(
        kernel,
        out_shape=outs,
        in_specs=specs or [VMEM] * len(ins),
        out_specs=VMEM if single else [VMEM] * len(outs),
        scratch_shapes=list(scratch),
        compiler_params=pltpu.CompilerParams(vmem_limit_bytes=mebibytes * 1024 * 1024),
        cost_estimate=pl.CostEstimate(
            flops=micros * 1000000, bytes_accessed=micros * 3000000, transcendentals=0
        ),
        name=name,
    )(*ins)


def shape(*dims, dtype=jnp.bfloat16):
    return jax.ShapeDtypeStruct(dims, dtype)


def scalar(value):
    return jnp.full((1,), value, jnp.int32)


def local(images, ctf, refs, shifts, lists, counts):
    f32, bf16 = jnp.float32, jnp.bfloat16
    parts, rdev, trans = images.shape[0], refs.shape[0], shifts.shape[0]
    refs_all = rdev * 16
    rows = 2 * trans * parts
    swap = [(0, 1), (1, 0)]
    core, x, y_lo = lax.axis_index("core"), lax.axis_index("x"), lax.axis_index("y_lo")
    z, y_hi = scalar(lax.axis_index("z")), scalar(lax.axis_index("y_hi"))
    ref = scalar(lax.axis_index(("z", "y_hi")))
    column = scalar(y_lo * 4 + x)
    core, x, y_lo = scalar(core), scalar(x), scalar(y_lo)

    mine = call(
        "pack", pack_kernel, [column, core, refs], shape(1, 2, HALF, LANES), [SMEM, SMEM, VMEM]
    )
    came = [over_z(mine, bits) for bits in (2, 4, 6)]
    half = shape(2, 4, parts, BLOCK)
    own, other = call(
        "weighted",
        weighted_kernel,
        [core, x, images, ctf, mine],
        [half, half],
        [SMEM, SMEM, VMEM, VMEM, ANY],
        micros=3,
    )
    evens = call(
        "stack",
        stack_kernel,
        [mine] + came + [own],
        shape(4, 2, HALF, LANES),
        [VMEM] * 4 + [ANY],
    )
    other = call("hold", stack_kernel, [other, evens], half, [VMEM, ANY])
    recv = lax.ppermute(other, "core", swap)
    slot = jnp.arange(lists.shape[1], dtype=jnp.int32)[None, :]
    used = jnp.where(slot < counts[:, None], lists, -1)
    used_pair = jnp.stack([used, lax.ppermute(used, "core", swap)])
    tables = [pltpu.VMEM((trans, CHUNK), f32)] * 2
    rots = []
    for first_xr in (0, 2):
        rots.append(
            call(
                "rotate",
                functools.partial(rotate_kernel, first_xr),
                [core, x, y_lo, shifts, own, recv],
                shape(2, 2, rows, BLOCK),
                [SMEM] * 3 + [VMEM] * 3,
                tables,
                8,
                3,
            )
        )
    blocks = call(
        "stack",
        stack_kernel,
        [evens, over_z(evens, 1), rots[0]],
        shape(8, 2, HALF, LANES),
        [VMEM, VMEM, ANY],
    )
    fours = [blocks] + [over(blocks, m, 1) for m in (1, 2, 3)]
    low, high = call(
        "join", join_kernel, fours + [rots[1]], [shape(2, 8, 2, HALF, LANES)] * 2, [VMEM] * 4 + [ANY]
    )
    one_low, three_high = over(low, 1, 0), over(high, 3, 0)
    one_high, three_low = over(high, 1, 0), over(low, 3, 0)
    two_low, two_high = over(one_low, 3, 0), over(three_high, 1, 0)
    lanes = -(-refs_all // LANES) * LANES
    scores = call(
        "forward",
        forward_kernel,
        [core, low, high, one_low, one_high, two_low, two_high, three_low, three_high]
        + rots,
        shape(rows, lanes, dtype=f32),
        [SMEM] + [VMEM] * 10,
        [pltpu.VMEM((2, refs_all, BLOCK), f32)],
        16,
        4,
    )
    theirs = lax.ppermute(scores, "core", swap)

    scale = (2 * ctf.shape[1]) ** -0.5
    part16, part32 = shape(32, HALF, LANES), shape(32, HALF, LANES, dtype=f32)
    more16, both16 = shape(33, HALF, LANES), shape(65, HALF, LANES)
    row = shape(8, LANES, dtype=f32)
    stays, to_one, to_three, one_high, three_low, evidence, totals = call(
        "backward",
        lambda *args: backward_kernel(scale, *args),
        [core, x, y_lo, z, y_hi, scores, theirs, used_pair, shifts, own, recv],
        [shape(4, 8, 2, HALF, LANES, dtype=f32), both16, both16, part32, part32]
        + [shape(parts, 1, dtype=f32), row],
        [SMEM] * 5 + [VMEM] * 6,
        [
            pltpu.VMEM((rows + 8, refs_all), f32),
            pltpu.VMEM((2, 2, rows, CHUNK), bf16),
            pltpu.VMEM((4, 4, 8, 2, HALF, LANES), f32),
            pltpu.VMEM((2, trans, CHUNK), f32),
            pltpu.VMEM((2, trans, CHUNK), f32),
        ],
        24,
        10,
    )
    from_one, from_three = over(to_one, 1, 0), over(to_three, 3, 0)
    one_high, three_low, both, third = call(
        "add",
        add_kernel,
        [totals, one_high, three_low, from_one, from_three],
        [more16, part16, row, row],
    )
    one_high, three_low = over(one_high, 1, 0), over(three_low, 3, 0)
    *middle, totals = call(
        "middle",
        middle_kernel,
        [both, third, stays, from_one, one_high, three_low, from_three],
        [shape(16, HALF, LANES, dtype=f32)] + [shape(17, HALF, LANES)] * 3 + [row],
    )
    came = [over(middle[m], m, 1) for m in (1, 2, 3)]
    even, odd, totals = call(
        "late",
        late_kernel,
        [totals, middle[0]] + came,
        [shape(8, HALF, LANES, dtype=f32), shape(9, HALF, LANES), row],
    )
    two32, three32 = shape(2, HALF, LANES, dtype=f32), shape(3, HALF, LANES, dtype=f32)
    own, *others, totals = call(
        "halve", halve_kernel, [totals, even, over_z(odd, 1)], [two32, three32, three32, three32, row]
    )
    others = [over_z(other, bits) for other, bits in zip(others, (2, 4, 6))]
    mine, give = call(
        "deal", deal_kernel, [core, totals, own] + others, [two32, two32], [SMEM] + [VMEM] * 5
    )
    came = lax.ppermute(give, "core", swap)
    result, totals = call(
        "last",
        last_kernel,
        [core, ref, mine, came],
        [shape(rdev, BLOCK, dtype=f32), shape(1, LANES, dtype=f32)],
        [SMEM, SMEM, VMEM, VMEM],
    )
    return (result, totals[0, :rdev], evidence[:, 0])


def solution(mesh):
    fine = Mesh(mesh.devices.reshape(2, 4, 2, 8, 2), EVERYONE)
    placed = (
        P(EVERYONE, None),
        P(EVERYONE, None),
        P(("z", "y_hi"), None),
        P(),
        P(EVERYONE, None),
        P(EVERYONE),
    )
    return jax.shard_map(
        local,
        mesh=fine,
        in_specs=placed,
        out_specs=(P(("z", "y_hi"), ("y_lo", "x", "core")), P(("z", "y_hi")), P(EVERYONE)),
        check_vma=False,
    )
```

```python
import functools
import math

import jax
import jax.numpy as jnp
from jax import lax
from jax.experimental import pallas as pl
from jax.experimental.pallas import tpu as pltpu
from jax.sharding import Mesh, PartitionSpec as P

GRID = 128
BLOCK = 1024
SIDE = BLOCK // 2
LANES = 128
GROUPS = SIDE // LANES
HALF = 48
CHUNK = 256
STACKED = (0, 4, 1, 5, 2, 6, 3, 7)
EVERYONE = ("y_lo", "x", "core", "z", "y_hi")
SMEM = pl.BlockSpec(memory_space=pltpu.SMEM)
VMEM = pl.BlockSpec(memory_space=pltpu.VMEM)
ANY = pl.BlockSpec(memory_space=pl.ANY)


def over_z(value, bits):
    return lax.ppermute(value, "z", [(i, i ^ bits) for i in range(8)])


def over(value, bits, core_on_x):
    pairs = []
    for y_lo in range(2):
        for x in range(4):
            for core in range(2):
                for y_hi in range(2):
                    here = ((y_lo * 4 + x) * 2 + core) * 2 + y_hi
                    if core == core_on_x:
                        there = ((y_lo * 4 + (x ^ bits)) * 2 + core) * 2 + y_hi
                    else:
                        there = (((y_lo ^ (bits & 1)) * 4 + x) * 2 + core) * 2 + (y_hi ^ (bits >> 1))
                    pairs.append((here, there))
    return lax.ppermute(value, ("y_lo", "x", "core", "y_hi"), pairs)


def pack_kernel(column_ref, core_ref, refs_ref, out_ref):
    for p in range(2):
        start = pl.multiple_of((2 * column_ref[0] + p) * BLOCK + core_ref[0] * SIDE, SIDE)
        block = refs_ref[:, pl.ds(start, SIDE)].astype(jnp.float32)
        tiles = [block[0:8, g * LANES : (g + 1) * LANES] for g in range(GROUPS)]
        tiles += [block[8:12, g * LANES : (g + 1) * LANES] for g in range(GROUPS)]
        out_ref[0, p] = jnp.concatenate(tiles, axis=0).astype(jnp.bfloat16)


def stack_kernel(*args):
    row = 0
    for ref in args[:-2]:
        count = ref.shape[0]
        args[-1][row : row + count] = ref[...]
        row += count


def join_kernel(own_ref, one_ref, two_ref, three_ref, rot_ref, low_ref, high_ref):
    low_ref[0] = own_ref[...]
    low_ref[1] = one_ref[...]
    high_ref[0] = two_ref[...]
    high_ref[1] = three_ref[...]


def weighted_kernel(core_ref, x_ref, images_ref, ctf_ref, before_ref, own_ref, other_ref):
    core, x = core_ref[0], x_ref[0]
    for out_ref, side in ((own_ref, core), (other_ref, 1 - core)):
        for xr in range(4):
            for p in range(2):
                column = pl.multiple_of((2 * (x ^ xr) + p) * BLOCK + side * SIDE, SIDE)
                gain = ctf_ref[:, pl.ds(column, SIDE)].astype(jnp.float32)
                for part in range(2):
                    start = pl.multiple_of(part * 8 * BLOCK + column, SIDE)
                    values = images_ref[:, pl.ds(start, SIDE)].astype(jnp.float32)
                    out_ref[part, xr, :, p * SIDE : (p + 1) * SIDE] = (gain * values).astype(
                        jnp.bfloat16
                    )


def rotate_kernel(first_xr, core_ref, x_ref, part_ref, shifts_ref, own_ref, recv_ref, *rest):
    *before, rot_ref, cos_ref, sin_ref = rest
    rows = own_ref.shape[2]
    trans = shifts_ref.shape[0]
    half = GRID // 2
    steps = BLOCK // CHUNK
    first = part_ref[0]
    for old_ref, new_ref in zip(before, (cos_ref, sin_ref)):
        new_ref[:first_xr] = old_ref[...]

    def step(index, carry):
        place = index // steps
        xr = first_xr + place
        start = pl.multiple_of((index % steps) * CHUNK, CHUNK)
        lanes = pl.ds(start, CHUNK)
        pixel = (2 * (x_ref[0] ^ xr) + start // SIDE) * BLOCK + core_ref[0] * SIDE + start % SIDE
        pixel = pixel + lax.broadcasted_iota(jnp.int32, (trans, CHUNK), 1)
        freq_y = (((pixel >> 6) + half) & (GRID - 1)) - half
        turns = (pixel & (half - 1)) * shifts_ref[:, 0:1] + freq_y * shifts_ref[:, 1:2]
        angle = (turns & (GRID - 1)).astype(jnp.float32) * jnp.float32(2.0 * math.pi / GRID)
        cos_ref[xr, :, lanes] = jnp.cos(angle)
        sin_ref[xr, :, lanes] = jnp.sin(angle)
        for h, half_ref in enumerate((own_ref, recv_ref)):
            re = half_ref[0, xr, :, lanes].astype(jnp.float32)
            im = half_ref[1, xr, :, lanes].astype(jnp.float32)
            for t in range(trans):
                cosine, sine = cos_ref[xr, t : t + 1, lanes], sin_ref[xr, t : t + 1, lanes]
                base = (h * trans + t) * rows
                rot_ref[first, place, base : base + rows, lanes] = (re * cosine + im * sine).astype(
                    jnp.bfloat16
                )
                rot_ref[1 - first, place, base : base + rows, lanes] = (
                    im * cosine - re * sine
                ).astype(jnp.bfloat16)
        return carry

    lax.fori_loop(0, rot_ref.shape[1] * steps, step, 0)


def three_parts(value):
    terms = []
    for _ in range(3):
        term = value.astype(jnp.bfloat16)
        terms.append(term.astype(jnp.float32))
        value = value - terms[-1]
    terms.append(jnp.zeros((HALF - 24, LANES), jnp.float32))
    return jnp.concatenate(terms, axis=0).astype(jnp.bfloat16)


def whole(block):
    block = block.astype(jnp.float32)
    return (block[0:8] + block[8:16]) + block[16:24]


def low_rows():
    return lax.broadcasted_iota(jnp.int32, (8, LANES), 0) < 4


def spread(own, other, wide_ref, row, column):
    low = low_rows()
    for g in range(GROUPS):
        lanes = slice(column + g * LANES, column + (g + 1) * LANES)
        wide_ref[row : row + 8, lanes] = own[8 * g : 8 * g + 8]
        wide_ref[row + 8 : row + 16, lanes] = other[8 * g : 8 * g + 8]
    for j in range(GROUPS // 2):
        at = 8 * (GROUPS + j)
        a, b = own[at : at + 8], other[at : at + 8]
        start = column + 2 * j * LANES
        wide_ref[row + 16 : row + 24, start : start + LANES] = jnp.where(low, a, pltpu.roll(b, 4, 0))
        start = start + LANES
        wide_ref[row + 16 : row + 24, start : start + LANES] = jnp.where(low, pltpu.roll(a, 4, 0), b)


def forward_kernel(*args):
    core_ref, blocks, rots, (out_ref, wide_ref) = args[0], args[1:9], args[9:11], args[11:]
    first = core_ref[0] == 0

    def block(n, m, k):
        return blocks[2 * n + m // 2][m % 2, STACKED[k]].astype(jnp.float32)

    for b in range(2):
        for xr in range(4):
            wide = wide_ref.at[xr % 2]
            for k in range(8):
                pair = []
                for a in range(2):
                    y = 2 * a + b
                    value = block(xr, y, k)
                    if y != xr:
                        value = jnp.where(first, value, block(y, xr, k))
                    pair.append(value)
                for p in range(2):
                    spread(pair[0][p], pair[1][p], wide, 24 * k, p * SIDE)
            product = lax.dot_general(
                rots[xr // 2][b, xr % 2],
                wide[...].astype(jnp.bfloat16),
                (((1,), (1,)), ((), ())),
                preferred_element_type=jnp.float32,
            )
            count = product.shape[1]
            if b == 0 and xr == 0:
                out_ref[:, :count] = product
                out_ref[:, count:] = jnp.zeros(
                    (product.shape[0], out_ref.shape[1] - count), jnp.float32
                )
            else:
                out_ref[:, :count] += product


def orientation(position, z, y_hi):
    k = jnp.zeros_like(position)
    for step in range(1, 8):
        k = k + (position >= 24 * step).astype(jnp.int32)
    place = position - 24 * k
    tail = (place >= 16).astype(jnp.int32)
    late = place - 16 * tail
    a = jnp.where(tail == 1, (late >= 4).astype(jnp.int32), (late >= 8).astype(jnp.int32))
    row = jnp.where(tail == 1, 8 + late - 4 * a, late - 8 * a)
    return ((z ^ k) * 2 + (y_hi ^ a)) * 12 + row


def softmax(scale, z, y_hi, mine_ref, theirs_ref, lists_ref, weights_ref, evidence_ref):
    particles, slots = lists_ref.shape[1:]
    refs_all = weights_ref.shape[1]
    trans = mine_ref.shape[0] // (2 * particles)
    shares = []
    index = orientation(lax.broadcasted_iota(jnp.int32, (8, refs_all), 1), z, y_hi)
    index = jnp.concatenate([index] * (particles // 8), axis=0)
    for h in range(2):
        listed = index == lists_ref[h, :, 0:1]
        for slot in range(1, slots):
            listed = listed | (index == lists_ref[h, :, slot : slot + 1])
        scores = []
        for t in range(trans):
            a = (h * trans + t) * particles
            b = ((1 - h) * trans + t) * particles
            value = mine_ref[a : a + particles, :refs_all] + theirs_ref[b : b + particles, :refs_all]
            scores.append(jnp.where(listed, value * scale, -jnp.inf))
        top = scores[0]
        for value in scores[1:]:
            top = jnp.maximum(top, value)
        top = jnp.max(top, axis=1, keepdims=True)
        exps = [jnp.exp(value - top) for value in scores]
        norm = exps[0]
        for value in exps[1:]:
            norm = norm + value
        summed = jnp.sum(norm, axis=1, keepdims=True)
        inverse = 1.0 / summed
        for t in range(trans):
            a = (h * trans + t) * particles
            weights_ref[a : a + particles] = exps[t] * inverse
        if h == 0:
            evidence_ref[...] = top + jnp.log(summed)
        shares.append(jnp.sum(norm * inverse, axis=0, keepdims=True))
    weights_ref[2 * trans * particles :] = jnp.broadcast_to(shares[0] + shares[1], (8, refs_all))


def weights_times_images(which, core, y_lo, weights, ins, rot_ref, sums_ref):
    cos_ref, sin_ref, own_ref, recv_ref = ins
    rows = own_ref.shape[2]
    trans = cos_ref.shape[1]
    low = low_rows()
    on_x = core == 0

    def step(at, carry):
        item, p = at // 2, at % 2
        far = item // 2
        xr = jnp.where(on_x, 1 + 2 * far if which else 2 - 2 * far, item)
        part = jnp.where(on_x, item % 2, which ^ y_lo)
        b = part ^ y_lo
        sign = (1 - 2 * part).astype(jnp.float32)
        for c in range(SIDE // CHUNK):
            lanes = pl.ds(pl.multiple_of(p * SIDE + c * CHUNK, CHUNK), CHUNK)
            for h, half_ref in enumerate((own_ref, recv_ref)):
                one = half_ref[part, xr, :, lanes].astype(jnp.float32)
                two = half_ref[1 - part, xr, :, lanes].astype(jnp.float32) * sign
                for t in range(trans):
                    cosine, sine = cos_ref[xr, t : t + 1, lanes], sin_ref[xr, t : t + 1, lanes]
                    base = (h * trans + t) * rows
                    rot_ref[c, base : base + rows, :] = (one * cosine + two * sine).astype(
                        jnp.bfloat16
                    )
            product = lax.dot_general(
                weights, rot_ref[c], (((1,), (0,)), ((), ())), preferred_element_type=jnp.float32
            )
            for a in range(2):
                i = jnp.where(on_x, far, a if which else 1 - a)
                j = jnp.where(on_x, 2 * a + b, xr)
                for k in range(8):
                    row = 24 * k
                    ref = sums_ref.at[i, j, k, p]
                    for g in range(2):
                        to = 8 * (2 * c + g)
                        ref[to : to + 8] = product[
                            row + 8 * a : row + 8 * a + 8, g * LANES : (g + 1) * LANES
                        ]
                    one = product[row + 16 : row + 24, :LANES]
                    two = product[row + 16 : row + 24, LANES:]
                    if a == 0:
                        tail = jnp.where(low, one, pltpu.roll(two, 4, 0))
                    else:
                        tail = jnp.where(low, pltpu.roll(one, 4, 0), two)
                    to = 8 * (GROUPS + c)
                    ref[to : to + 8] = tail
        return carry

    lax.fori_loop(0, 8, step, 0)


def first_kernel(scale, *args):
    core_ref, y_lo_ref, z_ref, y_hi_ref, mine_ref, theirs_ref, lists_ref = args[:7]
    ins, (stays, to_one, to_three, flipped_ref, evidence_ref, totals_ref) = args[7:11], args[11:17]
    weights_ref, rot_ref, sums_ref = args[17:]
    z, y_hi = z_ref[0], y_hi_ref[0]
    softmax(scale, z, y_hi, mine_ref, theirs_ref, lists_ref, weights_ref, evidence_ref)
    flipped = weights_ref[...].T
    refs_all, rows = flipped.shape[0], flipped.shape[1] - 8
    index = orientation(lax.broadcasted_iota(jnp.int32, (refs_all, 1), 0), z, y_hi)
    column = lax.broadcasted_iota(jnp.int32, (refs_all, refs_all), 1)
    totals = jnp.where(index == column, flipped[:, rows : rows + 1], 0.0)
    totals = jnp.sum(totals, axis=0, keepdims=True)
    totals_ref[...] = jnp.zeros(totals_ref.shape, jnp.float32)
    totals_ref[0:1, :] = totals[:, :LANES]
    totals_ref[1:2, : refs_all - LANES] = totals[:, LANES:]
    parts = three_parts(totals_ref[...])
    totals_ref[...] = whole(parts)
    to_one[32] = parts
    to_three[32] = parts
    weights = flipped[:, :rows].astype(jnp.bfloat16)
    flipped_ref[...] = weights
    weights_times_images(0, core_ref[0], y_lo_ref[0], weights, ins, rot_ref, sums_ref)
    for place in range(4):
        stays[place] = sums_ref[1, place]
        for k in range(4):
            for p in range(2):
                at = 8 * place + 2 * k + p
                to_one[at] = sums_ref[0, place, k, p].astype(jnp.bfloat16)
                to_three[at] = sums_ref[0, place, 4 + k, p].astype(jnp.bfloat16)


def second_kernel(core_ref, y_lo_ref, flipped_ref, *args):
    ins, (one_low, one_high, three_low, three_high), (rot_ref, sums_ref) = args[:4], args[4:8], args[8:]
    weights = flipped_ref[...]
    weights_times_images(1, core_ref[0], y_lo_ref[0], weights, ins, rot_ref, sums_ref)
    for place in range(4):
        for n, (low_ref, high_ref) in enumerate(((one_low, one_high), (three_low, three_high))):
            for k in range(4):
                for p in range(2):
                    at = 8 * place + 2 * k + p
                    low_ref[at] = sums_ref[n, place, k, p].astype(low_ref.dtype)
                    high_ref[at] = sums_ref[n, place, 4 + k, p].astype(high_ref.dtype)


def add_kernel(
    totals_ref, one_ref, three_ref, far_one, far_three, one_out, three_out, both_ref, third_ref
):
    one_out[0:32] = (one_ref[...] + far_three[0:32].astype(jnp.float32)).astype(jnp.bfloat16)
    one_out[32] = far_three[32]
    three_out[...] = (three_ref[...] + far_one[0:32].astype(jnp.float32)).astype(jnp.bfloat16)
    both_ref[...] = totals_ref[...] + whole(far_one[32])
    third_ref[...] = whole(far_three[32])


def middle_kernel(both_ref, third_ref, stays, one_low, one_high, three_low, three_high, *outs):
    totals_ref = outs[-1]
    totals = both_ref[...] + (whole(one_high[32]) + third_ref[...])
    parts = three_parts(totals)
    totals_ref[...] = whole(parts)
    for n, out_ref in enumerate(outs[:-1]):
        if n:
            out_ref[16] = parts
        for ks, one, three in ((0, one_low, three_low), (4, one_high, three_high)):
            for k in range(4):
                for p in range(2):
                    at = 8 * n + 2 * k + p
                    total = stays[n, ks + k, p] + one[at].astype(jnp.float32)
                    total = total + three[at].astype(jnp.float32)
                    out_ref[2 * (ks + k) + p] = total.astype(out_ref.dtype)


def late_kernel(totals_ref, stays, one, two, three, even_ref, odd_ref, sum_ref):
    totals = totals_ref[...] + whole(one[16])
    totals = totals + (whole(two[16]) + whole(three[16]))
    parts = three_parts(totals)
    sum_ref[...] = whole(parts)
    odd_ref[8] = parts
    for k in range(8):
        for p in range(2):
            at = 2 * k + p
            total = stays[at] + one[at].astype(jnp.float32)
            total = total + (two[at].astype(jnp.float32) + three[at].astype(jnp.float32))
            if k % 2 == 0:
                even_ref[2 * (k // 2) + p] = total
            else:
                odd_ref[2 * (k // 2) + p] = total.astype(odd_ref.dtype)


def halve_kernel(totals_ref, stays, came, own_ref, two_ref, four_ref, six_ref, sum_ref):
    totals = totals_ref[...] + whole(came[8])
    sum_ref[...] = totals
    for k, ref in enumerate((own_ref, two_ref, four_ref, six_ref)):
        for p in range(2):
            ref[p] = stays[2 * k + p] + came[2 * k + p].astype(jnp.float32)
        if k:
            ref[2] = jnp.zeros((HALF, LANES), jnp.float32)
            ref[2, 0:8] = totals


def deal_kernel(core_ref, totals_ref, stays, two, four, six, mine_ref, give_ref):
    first = core_ref[0] == 0
    low, high = [(stays[p] + two[p]) + (four[p] + six[p]) for p in range(2)]
    totals = (totals_ref[...] + two[2, 0:8]) + (four[2, 0:8] + six[2, 0:8])
    mine_ref[0] = jnp.where(first, low, high)
    give_ref[0] = jnp.where(first, high, low)
    for ref in (mine_ref, give_ref):
        ref[1] = jnp.zeros((HALF, LANES), jnp.float32)
        ref[1, 0:8] = totals


def last_kernel(core_ref, ref_ref, mine_ref, came_ref, out_ref, totals_ref):
    first = core_ref[0] == 0
    low = jnp.where(first, mine_ref[0], came_ref[0])
    high = jnp.where(first, came_ref[0], mine_ref[0])
    total = jnp.where(first, mine_ref[1, 0:8], came_ref[1, 0:8])
    row = jnp.concatenate([total[0:1], total[1:2]], axis=1)
    row = jnp.broadcast_to(row, (8, 2 * LANES))
    row = pltpu.roll(row, (2 * LANES - 12 * ref_ref[0]) % (2 * LANES), 1)
    totals_ref[...] = row[0:1, :LANES]
    for side, block in enumerate((low, high)):
        for g in range(GROUPS):
            start = side * SIDE + g * LANES
            out_ref[0:8, start : start + LANES] = block[8 * g : 8 * g + 8]
            at = 8 * GROUPS + 4 * g
            out_ref[8:12, start : start + LANES] = block[at : at + 4]


def call(name, kernel, ins, outs, specs=None, scratch=(), mebibytes=16, micros=1):
    single = not isinstance(outs, (list, tuple))
    return pl.pallas_call(
        kernel,
        out_shape=outs,
        in_specs=specs or [VMEM] * len(ins),
        out_specs=VMEM if single else [VMEM] * len(outs),
        scratch_shapes=list(scratch),
        compiler_params=pltpu.CompilerParams(vmem_limit_bytes=mebibytes * 1024 * 1024),
        cost_estimate=pl.CostEstimate(
            flops=micros * 1000000, bytes_accessed=micros * 3000000, transcendentals=0
        ),
        name=name,
    )(*ins)


def shape(*dims, dtype=jnp.bfloat16):
    return jax.ShapeDtypeStruct(dims, dtype)


def scalar(value):
    return jnp.full((1,), value, jnp.int32)


def local(images, ctf, refs, shifts, lists, counts):
    f32, bf16 = jnp.float32, jnp.bfloat16
    parts, rdev, trans = images.shape[0], refs.shape[0], shifts.shape[0]
    refs_all = rdev * 16
    rows = 2 * trans * parts
    swap = [(0, 1), (1, 0)]
    core, x, y_lo = lax.axis_index("core"), lax.axis_index("x"), lax.axis_index("y_lo")
    z, y_hi = scalar(lax.axis_index("z")), scalar(lax.axis_index("y_hi"))
    ref = scalar(lax.axis_index(("z", "y_hi")))
    column = scalar(y_lo * 4 + x)
    core, x, y_lo = scalar(core), scalar(x), scalar(y_lo)

    mine = call(
        "pack", pack_kernel, [column, core, refs], shape(1, 2, HALF, LANES), [SMEM, SMEM, VMEM]
    )
    came = [over_z(mine, bits) for bits in (2, 4, 6)]
    half = shape(2, 4, parts, BLOCK)
    own, other = call(
        "weighted",
        weighted_kernel,
        [core, x, images, ctf, mine],
        [half, half],
        [SMEM, SMEM, VMEM, VMEM, ANY],
        micros=3,
    )
    evens = call(
        "stack",
        stack_kernel,
        [mine] + came + [own],
        shape(4, 2, HALF, LANES),
        [VMEM] * 4 + [ANY],
    )
    other = call("hold", stack_kernel, [other, evens], half, [VMEM, ANY])
    recv = lax.ppermute(other, "core", swap)
    slot = jnp.arange(lists.shape[1], dtype=jnp.int32)[None, :]
    used = jnp.where(slot < counts[:, None], lists, -1)
    used_pair = jnp.stack([used, lax.ppermute(used, "core", swap)])
    rots, tables = [], []
    for first_xr in (0, 2):
        table = shape(first_xr + 2, trans, BLOCK, dtype=f32)
        rotated, *tables = call(
            "rotate",
            functools.partial(rotate_kernel, first_xr),
            [core, x, y_lo, shifts, own, recv] + tables,
            [shape(2, 2, rows, BLOCK), table, table],
            [SMEM] * 3 + [VMEM] * (3 + len(tables)),
            mebibytes=8,
            micros=3,
        )
        rots.append(rotated)
    blocks = call(
        "stack",
        stack_kernel,
        [evens, over_z(evens, 1), rots[0]],
        shape(8, 2, HALF, LANES),
        [VMEM, VMEM, ANY],
    )
    fours = [blocks] + [over(blocks, m, 1) for m in (1, 2, 3)]
    low, high = call(
        "join", join_kernel, fours + [rots[1]], [shape(2, 8, 2, HALF, LANES)] * 2, [VMEM] * 4 + [ANY]
    )
    one_low, three_high = over(low, 1, 0), over(high, 3, 0)
    one_high, three_low = over(high, 1, 0), over(low, 3, 0)
    two_low, two_high = over(one_low, 3, 0), over(three_high, 1, 0)
    lanes = -(-refs_all // LANES) * LANES
    scores = call(
        "forward",
        forward_kernel,
        [core, low, high, one_low, one_high, two_low, two_high, three_low, three_high]
        + rots,
        shape(rows, lanes, dtype=f32),
        [SMEM] + [VMEM] * 10,
        [pltpu.VMEM((2, refs_all, BLOCK), f32)],
        16,
        4,
    )
    theirs = lax.ppermute(scores, "core", swap)

    scale = (2 * ctf.shape[1]) ** -0.5
    part16, part32 = shape(32, HALF, LANES), shape(32, HALF, LANES, dtype=f32)
    more16, row = shape(33, HALF, LANES), shape(8, LANES, dtype=f32)
    ins = tables + [own, recv]
    scratch = [pltpu.VMEM((2, rows, CHUNK), bf16), pltpu.VMEM((2, 4, 8, 2, HALF, LANES), f32)]
    stays, to_one, to_three, flipped, evidence, totals = call(
        "first",
        functools.partial(first_kernel, scale),
        [core, y_lo, z, y_hi, scores, theirs, used_pair] + ins,
        [shape(4, 8, 2, HALF, LANES, dtype=f32), more16, more16, shape(refs_all, rows)]
        + [shape(parts, 1, dtype=f32), row],
        [SMEM] * 4 + [VMEM] * 7,
        [pltpu.VMEM((rows + 8, refs_all), f32)] + scratch,
        16,
        6,
    )
    far_one, far_three = over(to_one, 1, 0), over(to_three, 3, 0)
    one_low, one_high, three_low, three_high = call(
        "second",
        second_kernel,
        [core, y_lo, flipped] + ins,
        [part16, part32, part32, part16],
        [SMEM] * 2 + [VMEM] * 5,
        scratch,
        16,
        4,
    )
    one_low, three_high = over(one_low, 1, 0), over(three_high, 3, 0)
    one_high, three_low, both, third = call(
        "add",
        add_kernel,
        [totals, one_high, three_low, far_one, far_three],
        [more16, part16, row, row],
    )
    one_high, three_low = over(one_high, 1, 0), over(three_low, 3, 0)
    *middle, totals = call(
        "middle",
        middle_kernel,
        [both, third, stays, one_low, one_high, three_low, three_high],
        [shape(16, HALF, LANES, dtype=f32)] + [shape(17, HALF, LANES)] * 3 + [row],
    )
    came = [over(middle[m], m, 1) for m in (1, 2, 3)]
    even, odd, totals = call(
        "late",
        late_kernel,
        [totals, middle[0]] + came,
        [shape(8, HALF, LANES, dtype=f32), shape(9, HALF, LANES), row],
    )
    two32, three32 = shape(2, HALF, LANES, dtype=f32), shape(3, HALF, LANES, dtype=f32)
    own, *others, totals = call(
        "halve", halve_kernel, [totals, even, over_z(odd, 1)], [two32, three32, three32, three32, row]
    )
    others = [over_z(other, bits) for other, bits in zip(others, (2, 4, 6))]
    mine, give = call(
        "deal", deal_kernel, [core, totals, own] + others, [two32, two32], [SMEM] + [VMEM] * 5
    )
    came = lax.ppermute(give, "core", swap)
    result, totals = call(
        "last",
        last_kernel,
        [core, ref, mine, came],
        [shape(rdev, BLOCK, dtype=f32), shape(1, LANES, dtype=f32)],
        [SMEM, SMEM, VMEM, VMEM],
    )
    return (result, totals[0, :rdev], evidence[:, 0])


def solution(mesh):
    fine = Mesh(mesh.devices.reshape(2, 4, 2, 8, 2), EVERYONE)
    placed = (
        P(EVERYONE, None),
        P(EVERYONE, None),
        P(("z", "y_hi"), None),
        P(),
        P(EVERYONE, None),
        P(EVERYONE),
    )
    return jax.shard_map(
        local,
        mesh=fine,
        in_specs=placed,
        out_specs=(P(("z", "y_hi"), ("y_lo", "x", "core")), P(("z", "y_hi")), P(EVERYONE)),
        check_vma=False,
    )
```

```python
import functools
import math

import jax
import jax.numpy as jnp
from jax import lax
from jax.experimental import pallas as pl
from jax.experimental.pallas import tpu as pltpu
from jax.sharding import Mesh, PartitionSpec as P

GRID = 128
BLOCK = 1024
SIDE = BLOCK // 2
LANES = 128
GROUPS = SIDE // LANES
HALF = 48
CHUNK = 256
STACKED = (0, 4, 1, 5, 2, 6, 3, 7)
EVERYONE = ("y_lo", "x", "core", "z", "y_hi")
SMEM = pl.BlockSpec(memory_space=pltpu.SMEM)
VMEM = pl.BlockSpec(memory_space=pltpu.VMEM)
ANY = pl.BlockSpec(memory_space=pl.ANY)


def over_z(value, bits):
    return lax.ppermute(value, "z", [(i, i ^ bits) for i in range(8)])


def over(value, bits, core_on_x):
    pairs = []
    for y_lo in range(2):
        for x in range(4):
            for core in range(2):
                for y_hi in range(2):
                    here = ((y_lo * 4 + x) * 2 + core) * 2 + y_hi
                    if core == core_on_x:
                        there = ((y_lo * 4 + (x ^ bits)) * 2 + core) * 2 + y_hi
                    else:
                        there = (((y_lo ^ (bits & 1)) * 4 + x) * 2 + core) * 2 + (y_hi ^ (bits >> 1))
                    pairs.append((here, there))
    return lax.ppermute(value, ("y_lo", "x", "core", "y_hi"), pairs)


def pack_kernel(column_ref, core_ref, refs_ref, out_ref):
    for p in range(2):
        start = pl.multiple_of((2 * column_ref[0] + p) * BLOCK + core_ref[0] * SIDE, SIDE)
        block = refs_ref[:, pl.ds(start, SIDE)].astype(jnp.float32)
        tiles = [block[0:8, g * LANES : (g + 1) * LANES] for g in range(GROUPS)]
        tiles += [block[8:12, g * LANES : (g + 1) * LANES] for g in range(GROUPS)]
        out_ref[0, p] = jnp.concatenate(tiles, axis=0).astype(jnp.bfloat16)


def stack_kernel(*args):
    row = 0
    for ref in args[:-2]:
        count = ref.shape[0]
        args[-1][row : row + count] = ref[...]
        row += count


def join_kernel(own_ref, one_ref, two_ref, three_ref, rot_ref, low_ref, high_ref):
    low_ref[0] = own_ref[...]
    low_ref[1] = one_ref[...]
    high_ref[0] = two_ref[...]
    high_ref[1] = three_ref[...]


def weighted_kernel(core_ref, x_ref, images_ref, ctf_ref, before_ref, own_ref, other_ref):
    core, x = core_ref[0], x_ref[0]
    for out_ref, side in ((own_ref, core), (other_ref, 1 - core)):
        for xr in range(4):
            for p in range(2):
                column = pl.multiple_of((2 * (x ^ xr) + p) * BLOCK + side * SIDE, SIDE)
                gain = ctf_ref[:, pl.ds(column, SIDE)].astype(jnp.float32)
                for part in range(2):
                    start = pl.multiple_of(part * 8 * BLOCK + column, SIDE)
                    values = images_ref[:, pl.ds(start, SIDE)].astype(jnp.float32)
                    out_ref[part, xr, :, p * SIDE : (p + 1) * SIDE] = (gain * values).astype(
                        jnp.bfloat16
                    )


def rotate_kernel(first_xr, core_ref, x_ref, part_ref, shifts_ref, own_ref, recv_ref, *rest):
    *before, rot_ref, cos_ref, sin_ref = rest
    rows = own_ref.shape[2]
    trans = shifts_ref.shape[0]
    half = GRID // 2
    steps = BLOCK // CHUNK
    first = part_ref[0]
    for old_ref, new_ref in zip(before, (cos_ref, sin_ref)):
        new_ref[:first_xr] = old_ref[...]

    def step(index, carry):
        place = index // steps
        xr = first_xr + place
        start = pl.multiple_of((index % steps) * CHUNK, CHUNK)
        lanes = pl.ds(start, CHUNK)
        pixel = (2 * (x_ref[0] ^ xr) + start // SIDE) * BLOCK + core_ref[0] * SIDE + start % SIDE
        pixel = pixel + lax.broadcasted_iota(jnp.int32, (trans, CHUNK), 1)
        freq_y = (((pixel >> 6) + half) & (GRID - 1)) - half
        turns = (pixel & (half - 1)) * shifts_ref[:, 0:1] + freq_y * shifts_ref[:, 1:2]
        angle = (turns & (GRID - 1)).astype(jnp.float32) * jnp.float32(2.0 * math.pi / GRID)
        cos_ref[xr, :, lanes] = jnp.cos(angle)
        sin_ref[xr, :, lanes] = jnp.sin(angle)
        for h, half_ref in enumerate((own_ref, recv_ref)):
            re = half_ref[0, xr, :, lanes].astype(jnp.float32)
            im = half_ref[1, xr, :, lanes].astype(jnp.float32)
            for t in range(trans):
                cosine, sine = cos_ref[xr, t : t + 1, lanes], sin_ref[xr, t : t + 1, lanes]
                base = (h * trans + t) * rows
                rot_ref[first, place, base : base + rows, lanes] = (re * cosine + im * sine).astype(
                    jnp.bfloat16
                )
                rot_ref[1 - first, place, base : base + rows, lanes] = (
                    im * cosine - re * sine
                ).astype(jnp.bfloat16)
        return carry

    lax.fori_loop(0, rot_ref.shape[1] * steps, step, 0)


def three_parts(value):
    terms = []
    for _ in range(3):
        term = value.astype(jnp.bfloat16)
        terms.append(term.astype(jnp.float32))
        value = value - terms[-1]
    terms.append(jnp.zeros((HALF - 24, LANES), jnp.float32))
    return jnp.concatenate(terms, axis=0).astype(jnp.bfloat16)


def whole(block):
    block = block.astype(jnp.float32)
    return (block[0:8] + block[8:16]) + block[16:24]


def low_rows():
    return lax.broadcasted_iota(jnp.int32, (8, LANES), 0) < 4


def spread(own, other, wide_ref, row, column):
    low = low_rows()
    for g in range(GROUPS):
        lanes = slice(column + g * LANES, column + (g + 1) * LANES)
        wide_ref[row : row + 8, lanes] = own[8 * g : 8 * g + 8]
        wide_ref[row + 8 : row + 16, lanes] = other[8 * g : 8 * g + 8]
    for j in range(GROUPS // 2):
        at = 8 * (GROUPS + j)
        a, b = own[at : at + 8], other[at : at + 8]
        start = column + 2 * j * LANES
        wide_ref[row + 16 : row + 24, start : start + LANES] = jnp.where(low, a, pltpu.roll(b, 4, 0))
        start = start + LANES
        wide_ref[row + 16 : row + 24, start : start + LANES] = jnp.where(low, pltpu.roll(a, 4, 0), b)


def forward_kernel(*args):
    core_ref, blocks, rots, (out_ref, wide_ref) = args[0], args[1:9], args[9:11], args[11:]
    first = core_ref[0] == 0

    def block(n, m, k):
        return blocks[2 * n + m // 2][m % 2, STACKED[k]].astype(jnp.float32)

    for b in range(2):
        for xr in range(4):
            wide = wide_ref.at[xr % 2]
            for k in range(8):
                pair = []
                for a in range(2):
                    y = 2 * a + b
                    value = block(xr, y, k)
                    if y != xr:
                        value = jnp.where(first, value, block(y, xr, k))
                    pair.append(value)
                for p in range(2):
                    spread(pair[0][p], pair[1][p], wide, 24 * k, p * SIDE)
            product = lax.dot_general(
                rots[xr // 2][b, xr % 2],
                wide[...].astype(jnp.bfloat16),
                (((1,), (1,)), ((), ())),
                preferred_element_type=jnp.float32,
            )
            count = product.shape[1]
            if b == 0 and xr == 0:
                out_ref[:, :count] = product
                out_ref[:, count:] = jnp.zeros(
                    (product.shape[0], out_ref.shape[1] - count), jnp.float32
                )
            else:
                out_ref[:, :count] += product


def orientation(position, z, y_hi):
    k = jnp.zeros_like(position)
    for step in range(1, 8):
        k = k + (position >= 24 * step).astype(jnp.int32)
    place = position - 24 * k
    tail = (place >= 16).astype(jnp.int32)
    late = place - 16 * tail
    a = jnp.where(tail == 1, (late >= 4).astype(jnp.int32), (late >= 8).astype(jnp.int32))
    row = jnp.where(tail == 1, 8 + late - 4 * a, late - 8 * a)
    return ((z ^ k) * 2 + (y_hi ^ a)) * 12 + row


def softmax(scale, z, y_hi, mine_ref, theirs_ref, lists_ref, weights_ref, evidence_ref):
    particles, slots = lists_ref.shape[1:]
    refs_all = weights_ref.shape[1]
    trans = mine_ref.shape[0] // (2 * particles)
    shares = []
    index = orientation(lax.broadcasted_iota(jnp.int32, (8, refs_all), 1), z, y_hi)
    index = jnp.concatenate([index] * (particles // 8), axis=0)
    for h in range(2):
        listed = index == lists_ref[h, :, 0:1]
        for slot in range(1, slots):
            listed = listed | (index == lists_ref[h, :, slot : slot + 1])
        scores = []
        for t in range(trans):
            a = (h * trans + t) * particles
            b = ((1 - h) * trans + t) * particles
            value = mine_ref[a : a + particles, :refs_all] + theirs_ref[b : b + particles, :refs_all]
            scores.append(jnp.where(listed, value * scale, -jnp.inf))
        top = scores[0]
        for value in scores[1:]:
            top = jnp.maximum(top, value)
        top = jnp.max(top, axis=1, keepdims=True)
        exps = [jnp.exp(value - top) for value in scores]
        norm = exps[0]
        for value in exps[1:]:
            norm = norm + value
        summed = jnp.sum(norm, axis=1, keepdims=True)
        inverse = 1.0 / summed
        for t in range(trans):
            a = (h * trans + t) * particles
            weights_ref[a : a + particles] = exps[t] * inverse
        if h == 0:
            evidence_ref[...] = top + jnp.log(summed)
        shares.append(jnp.sum(norm * inverse, axis=0, keepdims=True))
    weights_ref[2 * trans * particles :] = jnp.broadcast_to(shares[0] + shares[1], (8, refs_all))


def weights_times_images(which, core, y_lo, weights, ins, rot_ref, sums_ref):
    cos_ref, sin_ref, own_ref, recv_ref = ins
    rows = own_ref.shape[2]
    trans = cos_ref.shape[1]
    low = low_rows()
    on_x = core == 0

    def step(at, carry):
        item, p = at // 2, at % 2
        far = item // 2
        xr = jnp.where(on_x, 1 + 2 * far if which else 2 - 2 * far, item)
        part = jnp.where(on_x, item % 2, which ^ y_lo)
        b = part ^ y_lo
        sign = (1 - 2 * part).astype(jnp.float32)
        for c in range(SIDE // CHUNK):
            lanes = pl.ds(pl.multiple_of(p * SIDE + c * CHUNK, CHUNK), CHUNK)
            for h, half_ref in enumerate((own_ref, recv_ref)):
                one = half_ref[part, xr, :, lanes].astype(jnp.float32)
                two = half_ref[1 - part, xr, :, lanes].astype(jnp.float32) * sign
                for t in range(trans):
                    cosine, sine = cos_ref[xr, t : t + 1, lanes], sin_ref[xr, t : t + 1, lanes]
                    base = (h * trans + t) * rows
                    rot_ref[c, base : base + rows, :] = (one * cosine + two * sine).astype(
                        jnp.bfloat16
                    )
            product = lax.dot_general(
                weights, rot_ref[c], (((1,), (0,)), ((), ())), preferred_element_type=jnp.float32
            )
            for a in range(2):
                i = jnp.where(on_x, far, a if which else 1 - a)
                j = jnp.where(on_x, 2 * a + b, xr)
                for k in range(8):
                    row = 24 * k
                    ref = sums_ref.at[i, j, k, p]
                    for g in range(2):
                        to = 8 * (2 * c + g)
                        ref[to : to + 8] = product[
                            row + 8 * a : row + 8 * a + 8, g * LANES : (g + 1) * LANES
                        ]
                    one = product[row + 16 : row + 24, :LANES]
                    two = product[row + 16 : row + 24, LANES:]
                    if a == 0:
                        tail = jnp.where(low, one, pltpu.roll(two, 4, 0))
                    else:
                        tail = jnp.where(low, pltpu.roll(one, 4, 0), two)
                    to = 8 * (GROUPS + c)
                    ref[to : to + 8] = tail
        return carry

    lax.fori_loop(0, 8, step, 0)


def first_kernel(scale, *args):
    core_ref, y_lo_ref, z_ref, y_hi_ref, mine_ref, theirs_ref, lists_ref = args[:7]
    ins, (stays, to_one, to_three, flipped_ref, evidence_ref, totals_ref) = args[7:11], args[11:17]
    weights_ref, rot_ref, sums_ref = args[17:]
    z, y_hi = z_ref[0], y_hi_ref[0]
    softmax(scale, z, y_hi, mine_ref, theirs_ref, lists_ref, weights_ref, evidence_ref)
    flipped = weights_ref[...].T
    refs_all, rows = flipped.shape[0], flipped.shape[1] - 8
    index = orientation(lax.broadcasted_iota(jnp.int32, (refs_all, 1), 0), z, y_hi)
    column = lax.broadcasted_iota(jnp.int32, (refs_all, refs_all), 1)
    totals = jnp.where(index == column, flipped[:, rows : rows + 1], 0.0)
    totals = jnp.sum(totals, axis=0, keepdims=True)
    totals_ref[...] = jnp.zeros(totals_ref.shape, jnp.float32)
    totals_ref[0:1, :] = totals[:, :LANES]
    totals_ref[1:2, : refs_all - LANES] = totals[:, LANES:]
    parts = three_parts(totals_ref[...])
    totals_ref[...] = whole(parts)
    to_one[32] = parts
    to_three[32] = parts
    weights = flipped[:, :rows].astype(jnp.bfloat16)
    flipped_ref[...] = weights
    weights_times_images(0, core_ref[0], y_lo_ref[0], weights, ins, rot_ref, sums_ref)
    for place in range(4):
        stays[place] = sums_ref[1, place]
        for k in range(4):
            for p in range(2):
                at = 8 * place + 2 * k + p
                to_one[at] = sums_ref[0, place, k, p].astype(jnp.bfloat16)
                to_three[at] = sums_ref[0, place, 4 + k, p].astype(jnp.bfloat16)


def second_kernel(core_ref, y_lo_ref, flipped_ref, *args):
    ins, (one_low, one_high, three_low, three_high), (rot_ref, sums_ref) = args[:4], args[4:8], args[8:]
    weights = flipped_ref[...]
    weights_times_images(1, core_ref[0], y_lo_ref[0], weights, ins, rot_ref, sums_ref)
    for place in range(4):
        for n, (low_ref, high_ref) in enumerate(((one_low, one_high), (three_low, three_high))):
            for k in range(4):
                for p in range(2):
                    at = 8 * place + 2 * k + p
                    low_ref[at] = sums_ref[n, place, k, p].astype(low_ref.dtype)
                    high_ref[at] = sums_ref[n, place, 4 + k, p].astype(high_ref.dtype)


def add_kernel(*args):
    totals_ref, one_low, one_high, three_low, three_high, far_one, far_three = args[:7]
    one_out, three_out, both_ref, third_ref = args[7:]
    one_out[0:32] = one_low[...]
    total = one_high[...] + far_three[0:32].astype(jnp.float32)
    one_out[32:64] = total.astype(jnp.bfloat16)
    one_out[64] = far_three[32]
    total = three_low[...] + far_one[0:32].astype(jnp.float32)
    three_out[0:32] = total.astype(jnp.bfloat16)
    three_out[32:64] = three_high[...]
    both_ref[...] = totals_ref[...] + whole(far_one[32])
    third_ref[...] = whole(far_three[32])


def middle_kernel(both_ref, third_ref, stays, one, three, *outs):
    totals_ref = outs[-1]
    totals = both_ref[...] + (whole(one[64]) + third_ref[...])
    parts = three_parts(totals)
    totals_ref[...] = whole(parts)
    for n, out_ref in enumerate(outs[:-1]):
        if n:
            out_ref[16] = parts
        for ks in (0, 4):
            for k in range(4):
                for p in range(2):
                    at = 8 * ks + 8 * n + 2 * k + p
                    total = stays[n, ks + k, p] + one[at].astype(jnp.float32)
                    total = total + three[at].astype(jnp.float32)
                    out_ref[2 * (ks + k) + p] = total.astype(out_ref.dtype)


def late_kernel(totals_ref, stays, one, two, three, even_ref, odd_ref, sum_ref):
    totals = totals_ref[...] + whole(one[16])
    totals = totals + (whole(two[16]) + whole(three[16]))
    parts = three_parts(totals)
    sum_ref[...] = whole(parts)
    odd_ref[8] = parts
    for k in range(8):
        for p in range(2):
            at = 2 * k + p
            total = stays[at] + one[at].astype(jnp.float32)
            total = total + (two[at].astype(jnp.float32) + three[at].astype(jnp.float32))
            if k % 2 == 0:
                even_ref[2 * (k // 2) + p] = total
            else:
                odd_ref[2 * (k // 2) + p] = total.astype(odd_ref.dtype)


def halve_kernel(totals_ref, stays, came, own_ref, two_ref, four_ref, six_ref, sum_ref):
    parts = three_parts(totals_ref[...] + whole(came[8]))
    sum_ref[...] = whole(parts)
    for k, ref in enumerate((own_ref, two_ref, four_ref, six_ref)):
        for p in range(2):
            total = stays[2 * k + p] + came[2 * k + p].astype(jnp.float32)
            ref[p] = total.astype(ref.dtype)
        if k:
            ref[2] = parts


def deal_kernel(core_ref, totals_ref, stays, two, four, six, mine_ref, give_ref):
    first = core_ref[0] == 0
    sides = []
    for p in range(2):
        total = stays[p] + two[p].astype(jnp.float32)
        sides.append(total + (four[p].astype(jnp.float32) + six[p].astype(jnp.float32)))
    low, high = sides
    totals = (totals_ref[...] + whole(two[2])) + (whole(four[2]) + whole(six[2]))
    mine_ref[0] = jnp.where(first, low, high)
    give_ref[0] = jnp.where(first, high, low)
    for ref in (mine_ref, give_ref):
        ref[1] = jnp.zeros((HALF, LANES), jnp.float32)
        ref[1, 0:8] = totals


def last_kernel(core_ref, ref_ref, mine_ref, came_ref, out_ref, totals_ref):
    first = core_ref[0] == 0
    low = jnp.where(first, mine_ref[0], came_ref[0])
    high = jnp.where(first, came_ref[0], mine_ref[0])
    total = jnp.where(first, mine_ref[1, 0:8], came_ref[1, 0:8])
    row = jnp.concatenate([total[0:1], total[1:2]], axis=1)
    row = jnp.broadcast_to(row, (8, 2 * LANES))
    row = pltpu.roll(row, (2 * LANES - 12 * ref_ref[0]) % (2 * LANES), 1)
    totals_ref[...] = row[0:1, :LANES]
    for side, block in enumerate((low, high)):
        for g in range(GROUPS):
            start = side * SIDE + g * LANES
            out_ref[0:8, start : start + LANES] = block[8 * g : 8 * g + 8]
            at = 8 * GROUPS + 4 * g
            out_ref[8:12, start : start + LANES] = block[at : at + 4]


def call(name, kernel, ins, outs, specs=None, scratch=(), mebibytes=16, micros=1):
    single = not isinstance(outs, (list, tuple))
    return pl.pallas_call(
        kernel,
        out_shape=outs,
        in_specs=specs or [VMEM] * len(ins),
        out_specs=VMEM if single else [VMEM] * len(outs),
        scratch_shapes=list(scratch),
        compiler_params=pltpu.CompilerParams(vmem_limit_bytes=mebibytes * 1024 * 1024),
        cost_estimate=pl.CostEstimate(
            flops=micros * 1000000, bytes_accessed=micros * 3000000, transcendentals=0
        ),
        name=name,
    )(*ins)


def shape(*dims, dtype=jnp.bfloat16):
    return jax.ShapeDtypeStruct(dims, dtype)


def scalar(value):
    return jnp.full((1,), value, jnp.int32)


def local(images, ctf, refs, shifts, lists, counts):
    f32, bf16 = jnp.float32, jnp.bfloat16
    parts, rdev, trans = images.shape[0], refs.shape[0], shifts.shape[0]
    refs_all = rdev * 16
    rows = 2 * trans * parts
    swap = [(0, 1), (1, 0)]
    core, x, y_lo = lax.axis_index("core"), lax.axis_index("x"), lax.axis_index("y_lo")
    z, y_hi = scalar(lax.axis_index("z")), scalar(lax.axis_index("y_hi"))
    ref = scalar(lax.axis_index(("z", "y_hi")))
    column = scalar(y_lo * 4 + x)
    core, x, y_lo = scalar(core), scalar(x), scalar(y_lo)

    mine = call(
        "pack", pack_kernel, [column, core, refs], shape(1, 2, HALF, LANES), [SMEM, SMEM, VMEM]
    )
    came = [over_z(mine, bits) for bits in (2, 4, 6)]
    half = shape(2, 4, parts, BLOCK)
    own, other = call(
        "weighted",
        weighted_kernel,
        [core, x, images, ctf, mine],
        [half, half],
        [SMEM, SMEM, VMEM, VMEM, ANY],
        micros=3,
    )
    evens = call(
        "stack",
        stack_kernel,
        [mine] + came + [own],
        shape(4, 2, HALF, LANES),
        [VMEM] * 4 + [ANY],
    )
    other = call("hold", stack_kernel, [other, evens], half, [VMEM, ANY])
    recv = lax.ppermute(other, "core", swap)
    slot = jnp.arange(lists.shape[1], dtype=jnp.int32)[None, :]
    used = jnp.where(slot < counts[:, None], lists, -1)
    used_pair = jnp.stack([used, lax.ppermute(used, "core", swap)])
    rots, tables = [], []
    for first_xr in (0, 2):
        table = shape(first_xr + 2, trans, BLOCK, dtype=f32)
        rotated, *tables = call(
            "rotate",
            functools.partial(rotate_kernel, first_xr),
            [core, x, y_lo, shifts, own, recv] + tables,
            [shape(2, 2, rows, BLOCK), table, table],
            [SMEM] * 3 + [VMEM] * (3 + len(tables)),
            mebibytes=8,
            micros=3,
        )
        rots.append(rotated)
    blocks = call(
        "stack",
        stack_kernel,
        [evens, over_z(evens, 1), rots[0]],
        shape(8, 2, HALF, LANES),
        [VMEM, VMEM, ANY],
    )
    fours = [blocks] + [over(blocks, m, 1) for m in (1, 2, 3)]
    low, high = call(
        "join", join_kernel, fours + [rots[1]], [shape(2, 8, 2, HALF, LANES)] * 2, [VMEM] * 4 + [ANY]
    )
    one_low, three_high = over(low, 1, 0), over(high, 3, 0)
    one_high, three_low = over(high, 1, 0), over(low, 3, 0)
    two_low, two_high = over(one_low, 3, 0), over(three_high, 1, 0)
    lanes = -(-refs_all // LANES) * LANES
    scores = call(
        "forward",
        forward_kernel,
        [core, low, high, one_low, one_high, two_low, two_high, three_low, three_high]
        + rots,
        shape(rows, lanes, dtype=f32),
        [SMEM] + [VMEM] * 10,
        [pltpu.VMEM((2, refs_all, BLOCK), f32)],
        16,
        4,
    )
    theirs = lax.ppermute(scores, "core", swap)

    scale = (2 * ctf.shape[1]) ** -0.5
    part16, part32 = shape(32, HALF, LANES), shape(32, HALF, LANES, dtype=f32)
    more16, row = shape(33, HALF, LANES), shape(8, LANES, dtype=f32)
    ins = tables + [own, recv]
    scratch = [pltpu.VMEM((2, rows, CHUNK), bf16), pltpu.VMEM((2, 4, 8, 2, HALF, LANES), f32)]
    stays, to_one, to_three, flipped, evidence, totals = call(
        "first",
        functools.partial(first_kernel, scale),
        [core, y_lo, z, y_hi, scores, theirs, used_pair] + ins,
        [shape(4, 8, 2, HALF, LANES, dtype=f32), more16, more16, shape(refs_all, rows)]
        + [shape(parts, 1, dtype=f32), row],
        [SMEM] * 4 + [VMEM] * 7,
        [pltpu.VMEM((rows + 8, refs_all), f32)] + scratch,
        16,
        6,
    )
    far_one, far_three = over(to_one, 1, 0), over(to_three, 3, 0)
    one_low, one_high, three_low, three_high = call(
        "second",
        second_kernel,
        [core, y_lo, flipped] + ins,
        [part16, part32, part32, part16],
        [SMEM] * 2 + [VMEM] * 5,
        scratch,
        16,
        4,
    )
    one, three, both, third = call(
        "add",
        add_kernel,
        [totals, one_low, one_high, three_low, three_high, far_one, far_three],
        [shape(65, HALF, LANES), shape(64, HALF, LANES), row, row],
    )
    one, three = over(one, 1, 0), over(three, 3, 0)
    *middle, totals = call(
        "middle",
        middle_kernel,
        [both, third, stays, one, three],
        [shape(16, HALF, LANES, dtype=f32)] + [shape(17, HALF, LANES)] * 3 + [row],
    )
    came = [over(middle[m], m, 1) for m in (1, 2, 3)]
    even, odd, totals = call(
        "late",
        late_kernel,
        [totals, middle[0]] + came,
        [shape(8, HALF, LANES, dtype=f32), shape(9, HALF, LANES), row],
    )
    two32, three16 = shape(2, HALF, LANES, dtype=f32), shape(3, HALF, LANES)
    own, *others, totals = call(
        "halve", halve_kernel, [totals, even, over_z(odd, 1)], [two32, three16, three16, three16, row]
    )
    others = [over_z(other, bits) for other, bits in zip(others, (2, 4, 6))]
    mine, give = call(
        "deal", deal_kernel, [core, totals, own] + others, [two32, two32], [SMEM] + [VMEM] * 5
    )
    came = lax.ppermute(give, "core", swap)
    result, totals = call(
        "last",
        last_kernel,
        [core, ref, mine, came],
        [shape(rdev, BLOCK, dtype=f32), shape(1, LANES, dtype=f32)],
        [SMEM, SMEM, VMEM, VMEM],
    )
    return (result, totals[0, :rdev], evidence[:, 0])


def solution(mesh):
    fine = Mesh(mesh.devices.reshape(2, 4, 2, 8, 2), EVERYONE)
    placed = (
        P(EVERYONE, None),
        P(EVERYONE, None),
        P(("z", "y_hi"), None),
        P(),
        P(EVERYONE, None),
        P(EVERYONE),
    )
    return jax.shard_map(
        local,
        mesh=fine,
        in_specs=placed,
        out_specs=(P(("z", "y_hi"), ("y_lo", "x", "core")), P(("z", "y_hi")), P(EVERYONE)),
        check_vma=False,
    )
```

```python
import functools
import math

import jax
import jax.numpy as jnp
from jax import lax
from jax.experimental import pallas as pl
from jax.experimental.pallas import tpu as pltpu
from jax.sharding import Mesh, PartitionSpec as P

GRID = 128
BLOCK = 1024
SIDE = BLOCK // 2
LANES = 128
GROUPS = SIDE // LANES
HALF = 48
CHUNK = 256
STACKED = (0, 4, 1, 5, 2, 6, 3, 7)
EVERYONE = ("y_lo", "x", "core", "z", "y_hi")
SMEM = pl.BlockSpec(memory_space=pltpu.SMEM)
VMEM = pl.BlockSpec(memory_space=pltpu.VMEM)
ANY = pl.BlockSpec(memory_space=pl.ANY)


def over_z(value, bits):
    return lax.ppermute(value, "z", [(i, i ^ bits) for i in range(8)])


def over(value, bits, core_on_x):
    pairs = []
    for y_lo in range(2):
        for x in range(4):
            for core in range(2):
                for y_hi in range(2):
                    here = ((y_lo * 4 + x) * 2 + core) * 2 + y_hi
                    if core == core_on_x:
                        there = ((y_lo * 4 + (x ^ bits)) * 2 + core) * 2 + y_hi
                    else:
                        there = (((y_lo ^ (bits & 1)) * 4 + x) * 2 + core) * 2 + (y_hi ^ (bits >> 1))
                    pairs.append((here, there))
    return lax.ppermute(value, ("y_lo", "x", "core", "y_hi"), pairs)


def pack_kernel(column_ref, core_ref, refs_ref, out_ref):
    for p in range(2):
        start = pl.multiple_of((2 * column_ref[0] + p) * BLOCK + core_ref[0] * SIDE, SIDE)
        block = refs_ref[:, pl.ds(start, SIDE)].astype(jnp.float32)
        tiles = [block[0:8, g * LANES : (g + 1) * LANES] for g in range(GROUPS)]
        tiles += [block[8:12, g * LANES : (g + 1) * LANES] for g in range(GROUPS)]
        out_ref[0, p] = jnp.concatenate(tiles, axis=0).astype(jnp.bfloat16)


def stack_kernel(*args):
    row = 0
    for ref in args[:-2]:
        count = ref.shape[0]
        args[-1][row : row + count] = ref[...]
        row += count


def join_kernel(own_ref, one_ref, two_ref, three_ref, rot_ref, lists_ref, low_ref, high_ref):
    low_ref[0] = own_ref[...]
    low_ref[1] = one_ref[...]
    high_ref[0] = two_ref[...]
    high_ref[1] = three_ref[...]


def weighted_kernel(core_ref, x_ref, images_ref, ctf_ref, before_ref, own_ref, other_ref):
    core, x = core_ref[0], x_ref[0]
    for out_ref, side in ((own_ref, core), (other_ref, 1 - core)):
        for xr in range(4):
            for p in range(2):
                column = pl.multiple_of((2 * (x ^ xr) + p) * BLOCK + side * SIDE, SIDE)
                gain = ctf_ref[:, pl.ds(column, SIDE)].astype(jnp.float32)
                for part in range(2):
                    start = pl.multiple_of(part * 8 * BLOCK + column, SIDE)
                    values = images_ref[:, pl.ds(start, SIDE)].astype(jnp.float32)
                    out_ref[part, xr, :, p * SIDE : (p + 1) * SIDE] = (gain * values).astype(
                        jnp.bfloat16
                    )


def rotate_kernel(first_xr, core_ref, x_ref, part_ref, shifts_ref, own_ref, recv_ref, *rest):
    *before, rot_ref, cos_ref, sin_ref = rest
    rows = own_ref.shape[2]
    trans = shifts_ref.shape[0]
    half = GRID // 2
    steps = BLOCK // CHUNK
    first = part_ref[0]
    for old_ref, new_ref in zip(before, (cos_ref, sin_ref)):
        new_ref[:first_xr] = old_ref[...]

    def step(index, carry):
        place = index // steps
        xr = first_xr + place
        start = pl.multiple_of((index % steps) * CHUNK, CHUNK)
        lanes = pl.ds(start, CHUNK)
        pixel = (2 * (x_ref[0] ^ xr) + start // SIDE) * BLOCK + core_ref[0] * SIDE + start % SIDE
        pixel = pixel + lax.broadcasted_iota(jnp.int32, (trans, CHUNK), 1)
        freq_y = (((pixel >> 6) + half) & (GRID - 1)) - half
        turns = (pixel & (half - 1)) * shifts_ref[:, 0:1] + freq_y * shifts_ref[:, 1:2]
        angle = (turns & (GRID - 1)).astype(jnp.float32) * jnp.float32(2.0 * math.pi / GRID)
        cos_ref[xr, :, lanes] = jnp.cos(angle)
        sin_ref[xr, :, lanes] = jnp.sin(angle)
        for h, half_ref in enumerate((own_ref, recv_ref)):
            re = half_ref[0, xr, :, lanes].astype(jnp.float32)
            im = half_ref[1, xr, :, lanes].astype(jnp.float32)
            for t in range(trans):
                cosine, sine = cos_ref[xr, t : t + 1, lanes], sin_ref[xr, t : t + 1, lanes]
                base = (h * trans + t) * rows
                rot_ref[first, place, base : base + rows, lanes] = (re * cosine + im * sine).astype(
                    jnp.bfloat16
                )
                rot_ref[1 - first, place, base : base + rows, lanes] = (
                    im * cosine - re * sine
                ).astype(jnp.bfloat16)
        return carry

    lax.fori_loop(0, rot_ref.shape[1] * steps, step, 0)


def three_parts(value):
    terms = []
    for _ in range(3):
        term = value.astype(jnp.bfloat16)
        terms.append(term.astype(jnp.float32))
        value = value - terms[-1]
    terms.append(jnp.zeros((HALF - 24, LANES), jnp.float32))
    return jnp.concatenate(terms, axis=0).astype(jnp.bfloat16)


def whole(block):
    block = block.astype(jnp.float32)
    return (block[0:8] + block[8:16]) + block[16:24]


def low_rows():
    return lax.broadcasted_iota(jnp.int32, (8, LANES), 0) < 4


def spread(own, other, wide_ref, row, column):
    low = low_rows()
    for g in range(GROUPS):
        lanes = slice(column + g * LANES, column + (g + 1) * LANES)
        wide_ref[row : row + 8, lanes] = own[8 * g : 8 * g + 8]
        wide_ref[row + 8 : row + 16, lanes] = other[8 * g : 8 * g + 8]
    for j in range(GROUPS // 2):
        at = 8 * (GROUPS + j)
        a, b = own[at : at + 8], other[at : at + 8]
        start = column + 2 * j * LANES
        wide_ref[row + 16 : row + 24, start : start + LANES] = jnp.where(low, a, pltpu.roll(b, 4, 0))
        start = start + LANES
        wide_ref[row + 16 : row + 24, start : start + LANES] = jnp.where(low, pltpu.roll(a, 4, 0), b)


def forward_kernel(*args):
    core_ref, blocks, rots, (out_ref, wide_ref) = args[0], args[1:9], args[9:11], args[11:]
    first = core_ref[0] == 0

    def block(n, m, k):
        return blocks[2 * n + m // 2][m % 2, STACKED[k]].astype(jnp.float32)

    for b in range(2):
        for xr in range(4):
            wide = wide_ref.at[xr % 2]
            for k in range(8):
                pair = []
                for a in range(2):
                    y = 2 * a + b
                    value = block(xr, y, k)
                    if y != xr:
                        value = jnp.where(first, value, block(y, xr, k))
                    pair.append(value)
                for p in range(2):
                    spread(pair[0][p], pair[1][p], wide, 24 * k, p * SIDE)
            product = lax.dot_general(
                rots[xr // 2][b, xr % 2],
                wide[...].astype(jnp.bfloat16),
                (((1,), (1,)), ((), ())),
                preferred_element_type=jnp.float32,
            )
            count = product.shape[1]
            if b == 0 and xr == 0:
                out_ref[:, :count] = product
                out_ref[:, count:] = jnp.zeros(
                    (product.shape[0], out_ref.shape[1] - count), jnp.float32
                )
            else:
                out_ref[:, :count] += product


def orientation(position, z, y_hi):
    k = jnp.zeros_like(position)
    for step in range(1, 8):
        k = k + (position >= 24 * step).astype(jnp.int32)
    place = position - 24 * k
    tail = (place >= 16).astype(jnp.int32)
    late = place - 16 * tail
    a = jnp.where(tail == 1, (late >= 4).astype(jnp.int32), (late >= 8).astype(jnp.int32))
    row = jnp.where(tail == 1, 8 + late - 4 * a, late - 8 * a)
    return ((z ^ k) * 2 + (y_hi ^ a)) * 12 + row


def softmax(scale, z, y_hi, mine_ref, theirs_ref, lists_ref, weights_ref, evidence_ref):
    particles, slots = lists_ref.shape[1:]
    refs_all = weights_ref.shape[1]
    trans = mine_ref.shape[0] // (2 * particles)
    shares = []
    index = orientation(lax.broadcasted_iota(jnp.int32, (8, refs_all), 1), z, y_hi)
    index = jnp.concatenate([index] * (particles // 8), axis=0)
    for h in range(2):
        listed = index == lists_ref[h, :, 0:1]
        for slot in range(1, slots):
            listed = listed | (index == lists_ref[h, :, slot : slot + 1])
        scores = []
        for t in range(trans):
            a = (h * trans + t) * particles
            b = ((1 - h) * trans + t) * particles
            value = mine_ref[a : a + particles, :refs_all] + theirs_ref[b : b + particles, :refs_all]
            scores.append(jnp.where(listed, value * scale, -jnp.inf))
        top = scores[0]
        for value in scores[1:]:
            top = jnp.maximum(top, value)
        top = jnp.max(top, axis=1, keepdims=True)
        exps = [jnp.exp(value - top) for value in scores]
        norm = exps[0]
        for value in exps[1:]:
            norm = norm + value
        summed = jnp.sum(norm, axis=1, keepdims=True)
        inverse = 1.0 / summed
        for t in range(trans):
            a = (h * trans + t) * particles
            weights_ref[a : a + particles] = exps[t] * inverse
        if h == 0:
            evidence_ref[...] = top + jnp.log(summed)
        shares.append(jnp.sum(norm * inverse, axis=0, keepdims=True))
    weights_ref[2 * trans * particles :] = jnp.broadcast_to(shares[0] + shares[1], (8, refs_all))


def weights_times_images(which, core, y_lo, weights, ins, rot_ref, sums_ref):
    cos_ref, sin_ref, own_ref, recv_ref = ins
    rows = own_ref.shape[2]
    trans = cos_ref.shape[1]
    low = low_rows()
    on_x = core == 0

    def step(at, carry):
        item, p = at // 2, at % 2
        far = item // 2
        xr = jnp.where(on_x, 1 + 2 * far if which else 2 - 2 * far, item)
        part = jnp.where(on_x, item % 2, which ^ y_lo)
        b = part ^ y_lo
        sign = (1 - 2 * part).astype(jnp.float32)
        for c in range(SIDE // CHUNK):
            lanes = pl.ds(pl.multiple_of(p * SIDE + c * CHUNK, CHUNK), CHUNK)
            for h, half_ref in enumerate((own_ref, recv_ref)):
                one = half_ref[part, xr, :, lanes].astype(jnp.float32)
                two = half_ref[1 - part, xr, :, lanes].astype(jnp.float32) * sign
                for t in range(trans):
                    cosine, sine = cos_ref[xr, t : t + 1, lanes], sin_ref[xr, t : t + 1, lanes]
                    base = (h * trans + t) * rows
                    rot_ref[c, base : base + rows, :] = (one * cosine + two * sine).astype(
                        jnp.bfloat16
                    )
            product = lax.dot_general(
                weights, rot_ref[c], (((1,), (0,)), ((), ())), preferred_element_type=jnp.float32
            )
            for a in range(2):
                i = jnp.where(on_x, far, a if which else 1 - a)
                j = jnp.where(on_x, 2 * a + b, xr)
                for k in range(8):
                    row = 24 * k
                    ref = sums_ref.at[i, j, k, p]
                    for g in range(2):
                        to = 8 * (2 * c + g)
                        ref[to : to + 8] = product[
                            row + 8 * a : row + 8 * a + 8, g * LANES : (g + 1) * LANES
                        ]
                    one = product[row + 16 : row + 24, :LANES]
                    two = product[row + 16 : row + 24, LANES:]
                    if a == 0:
                        tail = jnp.where(low, one, pltpu.roll(two, 4, 0))
                    else:
                        tail = jnp.where(low, pltpu.roll(one, 4, 0), two)
                    to = 8 * (GROUPS + c)
                    ref[to : to + 8] = tail
        return carry

    lax.fori_loop(0, 8, step, 0)


def first_kernel(scale, *args):
    core_ref, y_lo_ref, z_ref, y_hi_ref, mine_ref, theirs_ref, lists_ref = args[:7]
    ins, (stays, to_one, to_three, flipped_ref, evidence_ref, totals_ref) = args[7:11], args[11:17]
    weights_ref, rot_ref, sums_ref = args[17:]
    z, y_hi = z_ref[0], y_hi_ref[0]
    softmax(scale, z, y_hi, mine_ref, theirs_ref, lists_ref, weights_ref, evidence_ref)
    flipped = weights_ref[...].T
    refs_all, rows = flipped.shape[0], flipped.shape[1] - 8
    index = orientation(lax.broadcasted_iota(jnp.int32, (refs_all, 1), 0), z, y_hi)
    column = lax.broadcasted_iota(jnp.int32, (refs_all, refs_all), 1)
    totals = jnp.where(index == column, flipped[:, rows : rows + 1], 0.0)
    totals = jnp.sum(totals, axis=0, keepdims=True)
    totals_ref[...] = jnp.zeros(totals_ref.shape, jnp.float32)
    totals_ref[0:1, :] = totals[:, :LANES]
    totals_ref[1:2, : refs_all - LANES] = totals[:, LANES:]
    parts = three_parts(totals_ref[...])
    totals_ref[...] = whole(parts)
    to_one[32] = parts
    to_three[32] = parts
    weights = flipped[:, :rows].astype(jnp.bfloat16)
    flipped_ref[...] = weights
    weights_times_images(0, core_ref[0], y_lo_ref[0], weights, ins, rot_ref, sums_ref)
    for place in range(4):
        stays[place] = sums_ref[1, place]
        for k in range(4):
            for p in range(2):
                at = 8 * place + 2 * k + p
                to_one[at] = sums_ref[0, place, k, p].astype(jnp.bfloat16)
                to_three[at] = sums_ref[0, place, 4 + k, p].astype(jnp.bfloat16)


def second_kernel(core_ref, y_lo_ref, flipped_ref, *args):
    ins, (one_low, one_high, three_low, three_high), (rot_ref, sums_ref) = args[:4], args[4:8], args[8:]
    weights = flipped_ref[...]
    weights_times_images(1, core_ref[0], y_lo_ref[0], weights, ins, rot_ref, sums_ref)
    for place in range(4):
        for n, (low_ref, high_ref) in enumerate(((one_low, one_high), (three_low, three_high))):
            for k in range(4):
                for p in range(2):
                    at = 8 * place + 2 * k + p
                    low_ref[at] = sums_ref[n, place, k, p].astype(low_ref.dtype)
                    high_ref[at] = sums_ref[n, place, 4 + k, p].astype(high_ref.dtype)


def add_kernel(*args):
    totals_ref, one_low, one_high, three_low, three_high, far_one, far_three = args[:7]
    one_out, three_out, both_ref, third_ref = args[7:]
    one_out[0:32] = one_low[...]
    total = one_high[...] + far_three[0:32].astype(jnp.float32)
    one_out[32:64] = total.astype(jnp.bfloat16)
    one_out[64] = far_three[32]
    total = three_low[...] + far_one[0:32].astype(jnp.float32)
    three_out[0:32] = total.astype(jnp.bfloat16)
    three_out[32:64] = three_high[...]
    both_ref[...] = totals_ref[...] + whole(far_one[32])
    third_ref[...] = whole(far_three[32])


def middle_kernel(both_ref, third_ref, stays, one, three, *outs):
    totals_ref = outs[-1]
    totals = both_ref[...] + (whole(one[64]) + third_ref[...])
    parts = three_parts(totals)
    totals_ref[...] = whole(parts)
    for n, out_ref in enumerate(outs[:-1]):
        if n:
            out_ref[16] = parts
        for ks in (0, 4):
            for k in range(4):
                for p in range(2):
                    at = 8 * ks + 8 * n + 2 * k + p
                    total = stays[n, ks + k, p] + one[at].astype(jnp.float32)
                    total = total + three[at].astype(jnp.float32)
                    out_ref[2 * (ks + k) + p] = total.astype(out_ref.dtype)


def late_kernel(totals_ref, stays, one, two, three, even_ref, odd_ref, sum_ref):
    totals = totals_ref[...] + whole(one[16])
    totals = totals + (whole(two[16]) + whole(three[16]))
    parts = three_parts(totals)
    sum_ref[...] = whole(parts)
    odd_ref[8] = parts
    for k in range(8):
        for p in range(2):
            at = 2 * k + p
            total = stays[at] + one[at].astype(jnp.float32)
            total = total + (two[at].astype(jnp.float32) + three[at].astype(jnp.float32))
            if k % 2 == 0:
                even_ref[2 * (k // 2) + p] = total
            else:
                odd_ref[2 * (k // 2) + p] = total.astype(odd_ref.dtype)


def halve_kernel(totals_ref, stays, came, own_ref, two_ref, four_ref, six_ref, sum_ref):
    parts = three_parts(totals_ref[...] + whole(came[8]))
    sum_ref[...] = whole(parts)
    for k, ref in enumerate((own_ref, two_ref, four_ref, six_ref)):
        for p in range(2):
            total = stays[2 * k + p] + came[2 * k + p].astype(jnp.float32)
            ref[p] = total.astype(ref.dtype)
        if k:
            ref[2] = parts


def deal_kernel(core_ref, totals_ref, stays, two, four, six, mine_ref, give_ref):
    first = core_ref[0] == 0
    sides = []
    for p in range(2):
        total = stays[p] + two[p].astype(jnp.float32)
        sides.append(total + (four[p].astype(jnp.float32) + six[p].astype(jnp.float32)))
    low, high = sides
    totals = (totals_ref[...] + whole(two[2])) + (whole(four[2]) + whole(six[2]))
    mine_ref[0] = jnp.where(first, low, high)
    give_ref[0] = jnp.where(first, high, low)
    for ref in (mine_ref, give_ref):
        ref[1] = jnp.zeros((HALF, LANES), jnp.float32)
        ref[1, 0:8] = totals


def last_kernel(core_ref, ref_ref, mine_ref, came_ref, out_ref, totals_ref):
    first = core_ref[0] == 0
    low = jnp.where(first, mine_ref[0], came_ref[0])
    high = jnp.where(first, came_ref[0], mine_ref[0])
    total = jnp.where(first, mine_ref[1, 0:8], came_ref[1, 0:8])
    row = jnp.concatenate([total[0:1], total[1:2]], axis=1)
    row = jnp.broadcast_to(row, (8, 2 * LANES))
    row = pltpu.roll(row, (2 * LANES - 12 * ref_ref[0]) % (2 * LANES), 1)
    totals_ref[...] = row[0, : totals_ref.shape[0]]
    for side, block in enumerate((low, high)):
        for g in range(GROUPS):
            start = side * SIDE + g * LANES
            out_ref[0:8, start : start + LANES] = block[8 * g : 8 * g + 8]
            at = 8 * GROUPS + 4 * g
            out_ref[8:12, start : start + LANES] = block[at : at + 4]


def call(name, kernel, ins, outs, specs=None, scratch=(), mebibytes=16, micros=1):
    single = not isinstance(outs, (list, tuple))
    return pl.pallas_call(
        kernel,
        out_shape=outs,
        in_specs=specs or [VMEM] * len(ins),
        out_specs=VMEM if single else [VMEM] * len(outs),
        scratch_shapes=list(scratch),
        compiler_params=pltpu.CompilerParams(vmem_limit_bytes=mebibytes * 1024 * 1024),
        cost_estimate=pl.CostEstimate(
            flops=micros * 1000000, bytes_accessed=micros * 3000000, transcendentals=0
        ),
        name=name,
    )(*ins)


def shape(*dims, dtype=jnp.bfloat16):
    return jax.ShapeDtypeStruct(dims, dtype)


def scalar(value):
    return jnp.full((1,), value, jnp.int32)


def local(images, ctf, refs, shifts, lists, counts):
    f32, bf16 = jnp.float32, jnp.bfloat16
    parts, rdev, trans = images.shape[0], refs.shape[0], shifts.shape[0]
    refs_all = rdev * 16
    rows = 2 * trans * parts
    swap = [(0, 1), (1, 0)]
    core, x, y_lo = lax.axis_index("core"), lax.axis_index("x"), lax.axis_index("y_lo")
    z, y_hi = scalar(lax.axis_index("z")), scalar(lax.axis_index("y_hi"))
    ref = scalar(lax.axis_index(("z", "y_hi")))
    column = scalar(y_lo * 4 + x)
    core, x, y_lo = scalar(core), scalar(x), scalar(y_lo)

    mine = call(
        "pack", pack_kernel, [column, core, refs], shape(1, 2, HALF, LANES), [SMEM, SMEM, VMEM]
    )
    came = [over_z(mine, bits) for bits in (2, 4, 6)]
    half = shape(2, 4, parts, BLOCK)
    own, other = call(
        "weighted",
        weighted_kernel,
        [core, x, images, ctf, mine],
        [half, half],
        [SMEM, SMEM, VMEM, VMEM, ANY],
        micros=3,
    )
    evens = call(
        "stack",
        stack_kernel,
        [mine] + came + [own],
        shape(4, 2, HALF, LANES),
        [VMEM] * 4 + [ANY],
    )
    other = call("hold", stack_kernel, [other, evens], half, [VMEM, ANY])
    recv = lax.ppermute(other, "core", swap)
    slot = jnp.arange(lists.shape[1], dtype=jnp.int32)[None, :]
    used = jnp.where(slot < counts[:, None], lists, -1)
    used_pair = jnp.stack([used, lax.ppermute(used, "core", swap)])
    rots, tables = [], []
    for first_xr in (0, 2):
        table = shape(first_xr + 2, trans, BLOCK, dtype=f32)
        rotated, *tables = call(
            "rotate",
            functools.partial(rotate_kernel, first_xr),
            [core, x, y_lo, shifts, own, recv] + tables,
            [shape(2, 2, rows, BLOCK), table, table],
            [SMEM] * 3 + [VMEM] * (3 + len(tables)),
            mebibytes=8,
            micros=3,
        )
        rots.append(rotated)
    blocks = call(
        "stack",
        stack_kernel,
        [evens, over_z(evens, 1), rots[0]],
        shape(8, 2, HALF, LANES),
        [VMEM, VMEM, ANY],
    )
    fours = [blocks] + [over(blocks, m, 1) for m in (1, 2, 3)]
    low, high = call(
        "join",
        join_kernel,
        fours + [rots[1], used_pair],
        [shape(2, 8, 2, HALF, LANES)] * 2,
        [VMEM] * 4 + [ANY] * 2,
    )
    one_low, three_high = over(low, 1, 0), over(high, 3, 0)
    one_high, three_low = over(high, 1, 0), over(low, 3, 0)
    two_low, two_high = over(one_low, 3, 0), over(three_high, 1, 0)
    lanes = -(-refs_all // LANES) * LANES
    scores = call(
        "forward",
        forward_kernel,
        [core, low, high, one_low, one_high, two_low, two_high, three_low, three_high]
        + rots,
        shape(rows, lanes, dtype=f32),
        [SMEM] + [VMEM] * 10,
        [pltpu.VMEM((2, refs_all, BLOCK), f32)],
        16,
        4,
    )
    theirs = lax.ppermute(scores, "core", swap)

    scale = (2 * ctf.shape[1]) ** -0.5
    part16, part32 = shape(32, HALF, LANES), shape(32, HALF, LANES, dtype=f32)
    more16, row = shape(33, HALF, LANES), shape(8, LANES, dtype=f32)
    ins = tables + [own, recv]
    scratch = [pltpu.VMEM((2, rows, CHUNK), bf16), pltpu.VMEM((2, 4, 8, 2, HALF, LANES), f32)]
    stays, to_one, to_three, flipped, evidence, totals = call(
        "first",
        functools.partial(first_kernel, scale),
        [core, y_lo, z, y_hi, scores, theirs, used_pair] + ins,
        [shape(4, 8, 2, HALF, LANES, dtype=f32), more16, more16, shape(refs_all, rows)]
        + [shape(parts, 1, dtype=f32), row],
        [SMEM] * 4 + [VMEM] * 7,
        [pltpu.VMEM((rows + 8, refs_all), f32)] + scratch,
        16,
        6,
    )
    far_one, far_three = over(to_one, 1, 0), over(to_three, 3, 0)
    one_low, one_high, three_low, three_high = call(
        "second",
        second_kernel,
        [core, y_lo, flipped] + ins,
        [part16, part32, part32, part16],
        [SMEM] * 2 + [VMEM] * 5,
        scratch,
        16,
        4,
    )
    one, three, both, third = call(
        "add",
        add_kernel,
        [totals, one_low, one_high, three_low, three_high, far_one, far_three],
        [shape(65, HALF, LANES), shape(64, HALF, LANES), row, row],
    )
    one, three = over(one, 1, 0), over(three, 3, 0)
    *middle, totals = call(
        "middle",
        middle_kernel,
        [both, third, stays, one, three],
        [shape(16, HALF, LANES, dtype=f32)] + [shape(17, HALF, LANES)] * 3 + [row],
    )
    came = [over(middle[m], m, 1) for m in (1, 2, 3)]
    even, odd, totals = call(
        "late",
        late_kernel,
        [totals, middle[0]] + came,
        [shape(8, HALF, LANES, dtype=f32), shape(9, HALF, LANES), row],
    )
    two32, three16 = shape(2, HALF, LANES, dtype=f32), shape(3, HALF, LANES)
    own, *others, totals = call(
        "halve", halve_kernel, [totals, even, over_z(odd, 1)], [two32, three16, three16, three16, row]
    )
    others = [over_z(other, bits) for other, bits in zip(others, (2, 4, 6))]
    mine, give = call(
        "deal", deal_kernel, [core, totals, own] + others, [two32, two32], [SMEM] + [VMEM] * 5
    )
    came = lax.ppermute(give, "core", swap)
    result, totals = call(
        "last",
        last_kernel,
        [core, ref, mine, came],
        [shape(rdev, BLOCK, dtype=f32), shape(rdev, dtype=f32)],
        [SMEM, SMEM, VMEM, VMEM],
    )
    return (result, totals, evidence[:, 0])


def solution(mesh):
    fine = Mesh(mesh.devices.reshape(2, 4, 2, 8, 2), EVERYONE)
    placed = (
        P(EVERYONE, None),
        P(EVERYONE, None),
        P(("z", "y_hi"), None),
        P(),
        P(EVERYONE, None),
        P(EVERYONE),
    )
    return jax.shard_map(
        local,
        mesh=fine,
        in_specs=placed,
        out_specs=(P(("z", "y_hi"), ("y_lo", "x", "core")), P(("z", "y_hi")), P(EVERYONE)),
        check_vma=False,
    )
```
